128 devices in a mesh: row: 4 (over z), col: 32 (over y, x, core).
Axes of the slice: x: 4, y: 4, z: 4, core: 2. Of those that a mesh axis runs over, the one named last changes fastest.
Arguments:
- samples: bfloat16 [16, 4, 32, 8, 4096], P(None, 'row', 'col'), may hold values from -6 to 6
- ard_weight: float32 [4096], replicated, may hold values from 8.544922e-05 to 0.000769043, as said below
- nugget: bfloat16 [16, 4, 32, 8], P(None, 'row', 'col'), may hold values from 0.29882812 to 3
Outputs:
- factored: float32 [16, 4, 256, 2, 32, 256], P(None, 'row', None, None, 'col')
The draws below stay inside these ranges and needn't reach their ends.
Inputs may be any that keep to these rules, and one draw needn't show every extreme that they name: `ard_weight`: each weight is positive.
All inputs are finite; a program needn't handle non-finite values.
Results may differ from the reference program's by a relative error of at most 0.00046.
Values may be sent and summed in bfloat16 or wider, within the bound.
No kernel may reach another device: no remote copies, remote signals or barrier semaphores. Data moves between devices by JAX's collectives and lax.ppermute only.
A program may use at most 128 MiB of HBM per device.

```python
import math
import jax
import jax.numpy as jnp
from jax import lax

NB = 256
F = 4096
TC = 2
TR = 16
SUB = 8
N_ROW = 4
N_COL = 32


def draw_ard_weight(key, part):
    key = jax.random.fold_in(key, 11)
    scale_key, spread_key = jax.random.split(key)
    common = jnp.exp(jax.random.uniform(scale_key, (), jnp.float32, math.log(0.7), math.log(2.1))) / F
    spread = jax.random.uniform(spread_key, (F,), jnp.float32, 0.5, 1.5)
    return (common * spread).astype(jnp.float32)


def level_of(key, dims, shards, low, high):
    gain, own = 1.0, jax.random.fold_in(key, 6)
    for dim, shards_of in shards:
        draws = jnp.exp(jax.random.uniform(jax.random.fold_in(own, dim), (shards_of,), jnp.float32, low / len(shards), high / len(shards)))
        gain = gain * jnp.repeat(draws, dims[dim] // shards_of).reshape([-1 if axis == dim else 1 for axis in range(len(dims))])
    return gain


def normal_values(stream_key, dims, width, most, cuts=(), kind=jnp.bfloat16):
    entries = width * jax.random.normal(stream_key, dims, jnp.float32)
    if cuts:
        entries = entries * level_of(stream_key, dims, cuts, -0.22, 0.18)
    return jnp.clip(entries, -most, most).astype(kind)


def setup_inputs(seed: int = 0) -> dict:
    key_list = jax.random.split(jax.random.key(seed), 4)
    samples = normal_values(key_list[0], (TR, N_ROW, N_COL, SUB, F), 1.0, 6.0, ((1, 4), (2, 32)))
    ard_weight = draw_ard_weight(jax.random.fold_in(key_list[3], 71), 0)
    nugget = jnp.clip(jnp.exp(math.log(3.0) - 2.306499 * jax.random.uniform(key_list[2], (TR, N_ROW, N_COL, SUB), jnp.float32) ** level_of(key_list[2], (TR, N_ROW, N_COL, SUB), ((1, 4), (2, 32)), -0.2, 0.2)), 0.29882812, 3.0).astype(jnp.bfloat16)
    return dict(samples=samples, ard_weight=ard_weight, nugget=nugget)


def weighted_parts(row_side, ard_weight):
    widened = row_side.astype(jnp.float32)
    scaled = (widened * ard_weight).astype(jnp.bfloat16)
    sq_norms = jnp.sum(widened * widened * ard_weight, axis=1)
    return (scaled, sq_norms)

def reference(samples, ard_weight, nugget):
    order_total = TR * N_ROW * NB
    flat_rows = samples.reshape(order_total, F)
    diag_terms = nugget.reshape(order_total).astype(jnp.float32)
    scaled, sq_norms = weighted_parts(flat_rows, ard_weight)

    def tile_row(tile_index):
        offset = (tile_index * NB).astype(jnp.int32)
        part_rows = lax.dynamic_slice_in_dim(flat_rows, offset, NB, 0)
        part_norms = lax.dynamic_slice_in_dim(sq_norms, offset, NB, 0)
        cross_term = lax.dot_general(part_rows.astype(jnp.float32), scaled.astype(jnp.float32), (((1,), (1,)), ((), ())), preferred_element_type=jnp.float32)
        return jnp.exp(-0.5 * (part_norms[:, None] + sq_norms[None, :] - 2.0 * cross_term))
    kernel = lax.map(tile_row, jnp.arange(order_total // NB, dtype=jnp.int32)).reshape(order_total, order_total)
    diag_index = jnp.arange(order_total, dtype=jnp.int32)
    kernel = kernel.at[diag_index, diag_index].add(diag_terms)
    corner = jnp.linalg.cholesky(kernel[:NB, :NB])
    lower_panel = jax.scipy.linalg.solve_triangular(corner, kernel[NB:, :NB].T, lower=True).T
    panel_full = jnp.concatenate([corner, lower_panel], axis=0)
    update = kernel[NB:, NB:] - jnp.dot(lower_panel.astype(jnp.float32), lower_panel.T.astype(jnp.float32), precision=lax.Precision.HIGHEST, preferred_element_type=jnp.float32)
    factored = kernel.at[:, :NB].set(panel_full).at[NB:, NB:].set(update)
    return factored.reshape(TR, N_ROW, NB, TC, N_COL, NB)
```

```python
import functools

import jax
import jax.numpy as jnp
from jax import lax
from jax.experimental import pallas as pl
from jax.experimental.pallas import tpu as pltpu
from jax.sharding import PartitionSpec as P

NB = 256
HIGH = lax.Precision.HIGHEST
NT = (((1,), (1,)), ((), ()))
NN = (((1,), (0,)), ((), ()))


def dot_high(left, right, dims=NN):
    return lax.dot_general(left, right, dims, precision=HIGH, preferred_element_type=jnp.float32)


def eliminate(block):
    size = block.shape[0]
    height = 32
    rows = lax.broadcasted_iota(jnp.int32, (size, size), 0)
    cols = lax.broadcasted_iota(jnp.int32, (size, size), 1)
    eye = (rows == cols).astype(jnp.float32)
    whole = jnp.concatenate([block, eye], axis=1)
    parts = [whole[g * height : (g + 1) * height] for g in range(size // height)]
    inner = lax.broadcasted_iota(jnp.int32, (height, 1), 0)
    for j in range(size):
        first, at = divmod(j, height)
        pivot_row = parts[first][at : at + 1, :]
        pivot_row = pivot_row * (1.0 / pivot_row[:, j : j + 1])
        for g in range(first, size // height):
            factor = parts[g][:, j : j + 1]
            if g == first:
                factor = jnp.where(inner > at, factor, 0.0)
            parts[g] = parts[g] - factor * pivot_row
    whole = jnp.concatenate(parts, axis=0)
    pivots = jnp.sum(whole[:, :size] * eye, axis=1, keepdims=True)
    root = lax.rsqrt(pivots)
    root = root * (1.5 - 0.5 * pivots * root * root)
    return whole[:, size:] * root


def corner_kernel(a_ref, l_ref, x_ref):
    half = NB // 2
    rows = lax.broadcasted_iota(jnp.int32, (half, half), 0)
    cols = lax.broadcasted_iota(jnp.int32, (half, half), 1)
    lower = rows >= cols
    zero = jnp.zeros((half, half), jnp.float32)
    a11, a21, a22 = a_ref[:half, :half], a_ref[half:, :half], a_ref[half:, half:]
    x11 = eliminate(a11)
    l21 = dot_high(a21, x11, NT)
    l_ref[:half, :half] = jnp.where(lower, dot_high(a11, x11, NT), 0.0)
    l_ref[:half, half:] = zero
    l_ref[half:, :half] = l21
    s22 = a22 - dot_high(l21, l21, NT)
    x22 = eliminate(s22)
    l_ref[half:, half:] = jnp.where(lower, dot_high(s22, x22, NT), 0.0)
    x_ref[:half, :half] = x11
    x_ref[:half, half:] = zero
    x_ref[half:, :half] = -dot_high(x22, dot_high(l21, x11))
    x_ref[half:, half:] = x22


def factor_corner(corner_kernel_tile):
    shape = jax.ShapeDtypeStruct((NB, NB), jnp.float32)
    return pl.pallas_call(corner_kernel, out_shape=(shape, shape))(corner_kernel_tile)


def halves(value):
    high = value.astype(jnp.bfloat16)
    low = (value - high.astype(jnp.float32)).astype(jnp.bfloat16)
    return high, low


def main_kernel(tiles, rows_dev, where_ref, rows_ref, norm_ref, w_ref, wn_ref, nug_ref, inv_ref, q_ref, l_ref, o_ref):
    step = pl.program_id(0)
    row, col = where_ref[0], where_ref[1]
    eye = lax.broadcasted_iota(jnp.int32, (NB, NB), 0) == lax.broadcasted_iota(jnp.int32, (NB, NB), 1)
    for n in range(tiles):
        tile = (step * tiles + n) * rows_dev + row
        cross = lax.dot_general(
            rows_ref[n * NB : (n + 1) * NB, :], w_ref[...], NT, preferred_element_type=jnp.float32
        )
        norms = norm_ref[n * NB : (n + 1) * NB, :]
        kern = jnp.exp(-0.5 * (norms + wn_ref[...] - 2.0 * cross))
        left = kern[:, :NB] + jnp.where(eye & (tile == 0), nug_ref[:, :NB], 0.0)
        high, low = halves(left)
        panel = lax.dot_general(
            jnp.concatenate([high, high, low], axis=1), inv_ref[...], NN, preferred_element_type=jnp.float32
        )
        high, low = halves(panel)
        update = lax.dot_general(
            jnp.concatenate([high, high, low], axis=1), q_ref[...], NN, preferred_element_type=jnp.float32
        )
        first_tile = tile == 0
        for u in range(2):
            part = slice(NB * (u + 1), NB * (u + 2))
            own = kern[:, part] + jnp.where(eye & (tile == col + 32 * u), nug_ref[:, part], 0.0)
            result = jnp.where(first_tile, own, own - update[:, NB * u : NB * (u + 1)])
            if u == 0:
                result = jnp.where(col == 0, jnp.where(first_tile, l_ref[...], panel), result)
            for half in range(2):
                o_ref[pl.ds(n * NB * 4 + 2 * u + half, NB, stride=4), :] = result[:, 128 * half : 128 * (half + 1)]


def stacked(value):
    high = lax.reduce_precision(value, 8, 7)
    low = (value - high).astype(jnp.bfloat16)
    high = high.astype(jnp.bfloat16)
    return jnp.concatenate([high, low, high], axis=0)


def local(samples, ard_weight, nugget):
    row_count = lax.axis_size("row")
    col_count = lax.axis_size("col")
    row_index = lax.axis_index("row")
    col_index = lax.axis_index("col")
    row_tiles, _, _, sub, features = samples.shape
    quarter = features // row_count
    gathered = lax.all_gather(samples, "col", axis=2, tiled=True)

    own = samples.reshape(row_tiles, sub, features)
    widened = own.astype(jnp.float32)
    own_norms = jnp.sum(widened * widened * ard_weight, axis=2)
    n_high = lax.reduce_precision(own_norms, 8, 7)
    n_mid = lax.reduce_precision(own_norms - n_high, 8, 7)
    n_low = own_norms - n_high - n_mid
    pieces = jnp.stack([n_high, n_mid, n_low]).astype(jnp.bfloat16).transpose(0, 2, 1)

    cut = own.reshape(row_tiles, sub, row_count, quarter).transpose(2, 0, 1, 3)
    extra = jnp.broadcast_to(nugget.reshape(1, row_tiles, sub, 1), (row_count, row_tiles, sub, 128))
    sent = lax.all_to_all(jnp.concatenate([cut, extra], axis=3), "row", 0, 0)
    wide = quarter + 128
    fold = row_tiles // 2
    sent = sent.reshape(row_count, 2, fold, sub, wide)
    first = jnp.broadcast_to(sent[0, 0, 0][None, None], (col_count, 1, sub, wide))
    sent = sent.transpose(2, 0, 1, 3, 4).reshape(col_count, 2, sub, wide)
    sent = jnp.concatenate([first, sent], axis=1)
    tags = jnp.concatenate(
        [sent[..., quarter : quarter + 64],
         jnp.broadcast_to(pieces[None], (col_count, 3, sub, row_tiles)),
         sent[..., quarter + 80 :]], axis=3)
    sent = jnp.concatenate([sent[..., :quarter], tags], axis=3)
    got = lax.all_to_all(sent, "col", 0, 0)
    part = got[..., :quarter].transpose(1, 0, 2, 3).reshape(3 * NB, quarter)
    nug = got[..., quarter].astype(jnp.float32).transpose(1, 0, 2).reshape(1, 3 * NB)
    norm_bits = got[..., quarter + 64 : quarter + 80].astype(jnp.float32)
    row_norms = (norm_bits[:, 0] + norm_bits[:, 1]) + norm_bits[:, 2]
    row_norms = row_norms.transpose(2, 0, 1).reshape(row_tiles * NB, 1)

    up = [(i, (i + 1) % row_count) for i in range(row_count)]
    down = [(i, (i - 1) % row_count) for i in range(row_count)]
    mid = part.shape[0] // 2
    below = lax.ppermute(part, "row", up)
    above = lax.ppermute(part, "row", down)
    across = jnp.concatenate(
        [lax.ppermute(below[:mid], "row", up), lax.ppermute(above[mid:], "row", down)], axis=0
    )
    w_raw = jnp.zeros((3 * NB, features), jnp.bfloat16)
    for shift, value in enumerate((part, below, across, above)):
        at = lax.rem(row_index - shift + row_count, row_count) * quarter
        w_raw = lax.dynamic_update_slice(w_raw, value, (0, at))

    w_wide = w_raw.astype(jnp.float32)
    w_scaled = (w_wide * ard_weight).astype(jnp.bfloat16)
    w_norms = jnp.sum(w_wide * w_wide * ard_weight, axis=1)
    cross0 = lax.dot_general(w_raw, w_scaled[:NB], NT, preferred_element_type=jnp.float32)
    kern0 = jnp.exp(-0.5 * (w_norms[:, None] + w_norms[None, :NB] - 2.0 * cross0))
    tile0 = kern0[:NB] + jnp.diag(nug[0, :NB])
    corner, inverse = factor_corner(0.5 * (tile0 + tile0.T))
    q_panel = dot_high(inverse, kern0[NB:], NT)

    rows_data = gathered.reshape(row_tiles * NB, features)
    tiles = 2
    steps = row_tiles // tiles
    position = jnp.stack([row_index, col_index]).astype(jnp.int32)
    vmem = pl.BlockSpec(memory_space=pltpu.VMEM)
    flops = 2 * row_tiles * NB * 3 * NB * features
    result = pl.pallas_call(
        functools.partial(main_kernel, tiles, 4),
        out_shape=jax.ShapeDtypeStruct((row_tiles * NB * 4, 128), jnp.float32),
        grid_spec=pltpu.PrefetchScalarGridSpec(
            num_scalar_prefetch=1,
            grid=(steps,),
            in_specs=[
                pl.BlockSpec((tiles * NB, features), lambda i, _: (i, 0)),
                pl.BlockSpec((tiles * NB, 1), lambda i, _: (i, 0)),
                vmem, vmem, vmem, vmem, vmem, vmem,
            ],
            out_specs=pl.BlockSpec((tiles * NB * 4, 128), lambda i, _: (i, 0)),
        ),
        compiler_params=pltpu.CompilerParams(vmem_limit_bytes=48 * 2**20),
        cost_estimate=pl.CostEstimate(flops=flops, bytes_accessed=48 * 2**20, transcendentals=0),
    )(position, rows_data, row_norms, w_scaled, w_norms.reshape(1, -1), nug, stacked(inverse.T), stacked(q_panel), corner)
    return result.reshape(row_tiles, 1, NB, 2, 1, NB)


def solution(mesh):
    placed = (P(None, "row", "col", None, None), P(), P(None, "row", "col", None))
    return jax.shard_map(
        local,
        mesh=mesh,
        in_specs=placed,
        out_specs=P(None, "row", None, None, "col", None),
        check_vma=False,
    )
```

```python
import functools

import jax
import jax.numpy as jnp
from jax import lax
from jax.experimental import pallas as pl
from jax.experimental.pallas import tpu as pltpu
from jax.sharding import PartitionSpec as P

NB = 256
HIGH = lax.Precision.HIGHEST
NT = (((1,), (1,)), ((), ()))
NN = (((1,), (0,)), ((), ()))
RING = (0, 3, 1, 2)


def dot_high(left, right, dims=NN):
    return lax.dot_general(left, right, dims, precision=HIGH, preferred_element_type=jnp.float32)


def eliminate(block):
    size = block.shape[0]
    height = 32
    rows = lax.broadcasted_iota(jnp.int32, (size, size), 0)
    cols = lax.broadcasted_iota(jnp.int32, (size, size), 1)
    eye = (rows == cols).astype(jnp.float32)
    whole = jnp.concatenate([block, eye], axis=1)
    parts = [whole[g * height : (g + 1) * height] for g in range(size // height)]
    inner = lax.broadcasted_iota(jnp.int32, (height, 1), 0)
    for j in range(0, size, 2):
        first, at = divmod(j, height)
        row0 = parts[first][at : at + 1, :]
        row1 = parts[first][at + 1 : at + 2, :]
        a, b = row0[:, j : j + 1], row0[:, j + 1 : j + 2]
        c, d = row1[:, j : j + 1], row1[:, j + 1 : j + 2]
        inv_a = 1.0 / a
        scale = c * inv_a
        inv_d = 1.0 / (d - scale * b)
        row1 = row1 - scale * row0
        for g in range(first, size // height):
            f0 = parts[g][:, j : j + 1] * inv_a
            f1 = (parts[g][:, j + 1 : j + 2] - f0 * b) * inv_d
            if g == first:
                f0 = jnp.where(inner > at, f0, 0.0)
                f1 = jnp.where(inner > at + 1, f1, 0.0)
            parts[g] = parts[g] - f0 * row0 - f1 * row1
    whole = jnp.concatenate(parts, axis=0)
    pivots = jnp.sum(whole[:, :size] * eye, axis=1, keepdims=True)
    root = lax.rsqrt(pivots)
    root = root * (1.5 - 0.5 * pivots * root * root)
    return whole[:, size:] * root


def corner_kernel(a_ref, l_ref, x_ref):
    half = NB // 2
    rows = lax.broadcasted_iota(jnp.int32, (half, half), 0)
    cols = lax.broadcasted_iota(jnp.int32, (half, half), 1)
    lower = rows >= cols
    zero = jnp.zeros((half, half), jnp.float32)
    a11, a21, a22 = a_ref[:half, :half], a_ref[half:, :half], a_ref[half:, half:]
    x11 = eliminate(a11)
    l21 = dot_high(a21, x11, NT)
    l_ref[:half, :half] = jnp.where(lower, dot_high(a11, x11, NT), 0.0)
    l_ref[:half, half:] = zero
    l_ref[half:, :half] = l21
    s22 = a22 - dot_high(l21, l21, NT)
    x22 = eliminate(s22)
    l_ref[half:, half:] = jnp.where(lower, dot_high(s22, x22, NT), 0.0)
    x_ref[:half, :half] = x11
    x_ref[:half, half:] = zero
    x_ref[half:, :half] = -dot_high(x22, dot_high(l21, x11))
    x_ref[half:, half:] = x22


def factor_corner(tile):
    shape = jax.ShapeDtypeStruct((NB, NB), jnp.float32)
    return pl.pallas_call(
        corner_kernel,
        out_shape=(shape, shape),
        cost_estimate=pl.CostEstimate(flops=10**10, bytes_accessed=2**20, transcendentals=0),
    )(tile)


def halves(value):
    high = value.astype(jnp.bfloat16)
    low = (value - high.astype(jnp.float32)).astype(jnp.bfloat16)
    return high, low


def main_kernel(cuts, a_count, where_ref, norm_ref, grow_ref, *refs):
    count = len(cuts)
    pieces = refs[:count]
    w0_ref, wc_ref, wn_ref, nug_ref, gcol_ref, inv_ref, q_ref, l_ref = refs[count : count + 8]
    own_ref, sib_ref, rows_buf, w_buf, row_sem, w_sem = refs[count + 8 :]
    step = pl.program_id(0)
    row, col = where_ref[0], where_ref[1]

    def w_copy(n):
        if n == 0:
            return pltpu.make_async_copy(w0_ref, w_buf.at[0], w_sem.at[0])
        return pltpu.make_async_copy(wc_ref.at[n - 1], w_buf.at[n], w_sem.at[n])

    def row_copy(n):
        index, start, size = cuts[n]
        return pltpu.make_async_copy(pieces[n], rows_buf.at[index, pl.ds(start, size)], row_sem.at[n])

    @pl.when(step == 0)
    def _():
        for n in range(count):
            if cuts[n][0] == 0:
                row_copy(n).start()
        for n in range(5):
            w_copy(n).start()
        for n in range(count):
            if cuts[n][0] != 0:
                row_copy(n).start()

    for n in range(count):
        @pl.when(step == cuts[n][0])
        def _(n=n):
            row_copy(n).wait()

    def wait_w(n):
        @pl.when(step == 0)
        def _():
            w_copy(n).wait()

    norms = norm_ref[...]
    grow = grow_ref[...]

    def kern(n):
        part = slice(NB * n, NB * (n + 1))
        wait_w(n)
        cross = lax.dot_general(rows_buf[step], w_buf[n], NT, preferred_element_type=jnp.float32)
        value = jnp.exp(-0.5 * (norms + wn_ref[:, part] - 2.0 * cross))
        return value + jnp.where(grow == gcol_ref[:, part], nug_ref[:, part], 0.0)

    high, low = halves(kern(0))
    panel = lax.dot_general(
        jnp.concatenate([high, high, low], axis=1), inv_ref[...], NN, preferred_element_type=jnp.float32
    )
    high, low = halves(panel)
    triple = jnp.concatenate([high, high, low], axis=1)
    for n in range(1, 5):
        out_ref = own_ref if n < 3 else sib_ref
        owner = col if n < 3 else col + 1 - 2 * lax.rem(col, 2)
        u = (n - 1) % 2
        own = kern(n)
        update = lax.dot_general(
            triple, q_ref[:, NB * (n - 1) : NB * n], NN, preferred_element_type=jnp.float32
        )
        result = jnp.where(grow < NB, own, own - update)
        if u == 0:
            result = jnp.where(owner == 0, panel, result)
        for half in range(2):
            out_ref[0, pl.ds(2 * u + half, NB, stride=4), :] = result[:, 128 * half : 128 * (half + 1)]
        if u == 0:
            @pl.when((owner == 0) & (row == 0) & (step < a_count))
            def _(out_ref=out_ref):
                for d in range(4):
                    chip = where_ref[2 + 4 * step + d]
                    start = pl.multiple_of(chip * 16 + lax.rem(col, 2) * 8, 8)
                    tile = l_ref[pl.ds(start, 8), :]
                    for half in range(2):
                        out_ref[0, pl.ds(d * 64 * 4 + half, 8, stride=4), :] = tile[:, 128 * half : 128 * (half + 1)]


def run_main(pieces, cuts, a_count, where, norms, grow, rest):
    steps = max(cut[0] for cut in cuts) + 1
    shape = jax.ShapeDtypeStruct((steps, NB * 4, 128), jnp.float32)
    vmem = pl.BlockSpec(memory_space=pltpu.VMEM)
    hbm = pl.BlockSpec(memory_space=pl.ANY)
    features = pieces[0].shape[-1]
    column = pl.BlockSpec((NB, 1), lambda i, _: (i, 0))
    out = pl.BlockSpec((1, NB * 4, 128), lambda i, _: (i, 0, 0))
    return pl.pallas_call(
        functools.partial(main_kernel, cuts, a_count),
        out_shape=(shape, shape),
        grid_spec=pltpu.PrefetchScalarGridSpec(
            num_scalar_prefetch=1,
            grid=(steps,),
            in_specs=[column, column] + [hbm] * (len(pieces) + 2) + [vmem] * 6,
            out_specs=(out, out),
            scratch_shapes=[
                pltpu.VMEM((steps, NB, features), jnp.bfloat16),
                pltpu.VMEM((5, NB, features), jnp.bfloat16),
                pltpu.SemaphoreType.DMA((len(pieces),)),
                pltpu.SemaphoreType.DMA((5,)),
            ],
        ),
        compiler_params=pltpu.CompilerParams(vmem_limit_bytes=50 * 2**20),
        cost_estimate=pl.CostEstimate(
            flops=2 * steps * NB * 5 * NB * features, bytes_accessed=steps * 4 * 2**20, transcendentals=0
        ),
    )(where, norms, grow, *pieces, *rest)


def place_kernel(plan, where_ref, *refs):
    count = len(plan)
    sources, out_ref, sem = refs[:count], refs[-2], refs[-1]
    core = lax.rem(where_ref[1], 2)
    copies = []
    for source, (mine, kinds) in zip(sources, plan):
        side = core if mine else 1 - core
        for i, (is_a, first) in enumerate(kinds):
            for d in range(4):
                chip = where_ref[2 + 4 * first + d]
                copies.append(pltpu.make_async_copy(
                    source.at[i, d], out_ref.at[pl.ds(0 if is_a else 8, 8), chip, side], sem.at[len(copies)]))
    for copy in copies:
        copy.start()
    for copy in copies:
        copy.wait()


def place(sources, plan, where, before, shape):
    hbm = pl.BlockSpec(memory_space=pl.ANY)
    total = sum(4 * len(kinds) for _, kinds in plan)
    args = [where] + list(sources) + ([] if before is None else [before])
    return pl.pallas_call(
        functools.partial(place_kernel, plan),
        out_shape=jax.ShapeDtypeStruct(shape, jnp.float32),
        in_specs=[pl.BlockSpec(memory_space=pltpu.SMEM)] + [hbm] * (len(args) - 1),
        out_specs=hbm,
        scratch_shapes=[pltpu.SemaphoreType.DMA((total,))],
        input_output_aliases={} if before is None else {len(args) - 1: 0},
        cost_estimate=pl.CostEstimate(flops=0, bytes_accessed=total * 2**18, transcendentals=0),
    )(*args)


def stacked(value):
    high = lax.reduce_precision(value, 8, 7)
    low = (value - high).astype(jnp.bfloat16)
    high = high.astype(jnp.bfloat16)
    return jnp.concatenate([high, low, high], axis=0)


def rolled(value, axis, shift):
    double = jnp.concatenate([value, value], axis=axis)
    turned = lax.dynamic_slice_in_dim(double, shift, 4, axis)
    return jnp.concatenate([lax.slice_in_dim(turned, d, d + 1, axis=axis) for d in RING], axis=axis)


def x_move(step):
    return [(y * 8 + x * 2 + k, y * 8 + (x + step) % 4 * 2 + k) for y in range(4) for x in range(4) for k in range(2)]


def y_move(step):
    return [(y * 8 + x * 2 + k, (y + step) % 4 * 8 + x * 2 + k) for y in range(4) for x in range(4) for k in range(2)]


def local(samples, ard_weight, nugget):
    row_count = lax.axis_size("row")
    col_count = lax.axis_size("col")
    row_index = lax.axis_index("row")
    col_index = lax.axis_index("col")
    core = col_index % 2
    chip_x, chip_y = col_index // 2 % 4, col_index // 8
    row_tiles, _, _, sub, features = samples.shape
    quarter = features // row_count
    eighth = quarter // 2
    fold = row_tiles // 2
    own = samples.reshape(row_tiles, sub, features)
    sibling = [(i, i ^ 1) for i in range(col_count)]

    def swap(value):
        return lax.ppermute(value, "col", sibling)

    def ring(value, moves, cut):
        up, down = moves(1), moves(-1)
        below = lax.ppermute(value, "col", up)
        above = lax.ppermute(value, "col", down)
        far0 = lax.ppermute(below[:cut], "col", up)
        far1 = lax.ppermute(above[cut:], "col", down)
        return below, above, far0, far1

    part_a, part_b = own[:fold], own[fold:]
    line_a = ring(part_a, x_move, fold // 2)
    line_b = ring(part_b, y_move, fold // 2)
    four_a = jnp.concatenate([part_a, *line_a], axis=0).reshape(4, fold * sub, features)
    four_b = jnp.concatenate([part_b, *line_b], axis=0).reshape(4, fold * sub, features)
    grid_a = ring(four_a, y_move, 2)
    grid_b = ring(four_b, x_move, 2)

    widened = own.astype(jnp.float32)
    own_norms = jnp.sum(widened * widened * ard_weight, axis=2)
    n_high = lax.reduce_precision(own_norms, 8, 7)
    n_mid = lax.reduce_precision(own_norms - n_high, 8, 7)
    n_low = own_norms - n_high - n_mid
    bits = jnp.stack([n_high, n_mid, n_low]).astype(jnp.bfloat16).transpose(2, 0, 1).reshape(sub, 3 * row_tiles)

    cut = own.reshape(row_tiles, sub, row_count, quarter).transpose(2, 0, 1, 3)
    extra = jnp.broadcast_to(nugget.reshape(1, row_tiles, sub, 1), (row_count, row_tiles, sub, 128))
    sent = lax.all_to_all(jnp.concatenate([cut, extra], axis=3), "row", 0, 0)
    sent = sent.reshape(row_count, 2, fold, sub, quarter + 128).transpose(2, 0, 1, 3, 4)
    sent = sent.reshape(col_count, 2, sub, quarter + 128)
    body = sent[..., :quarter]
    tags = sent[..., quarter]
    first = body[0, 0]
    first = jnp.broadcast_to(
        jnp.stack([first[:, :eighth], first[:, eighth:]])[None], (col_count // 2, 2, sub, eighth)
    ).reshape(col_count, sub, eighth)
    tail = jnp.concatenate(
        [jnp.broadcast_to(tags[0, 0][None, :, None], (col_count, sub, 1)),
         tags[:, 0, :, None], tags[:, 1, :, None],
         jnp.zeros((col_count, sub, 61), jnp.bfloat16),
         jnp.broadcast_to(bits[None], (col_count, sub, 3 * row_tiles)),
         jnp.zeros((col_count, sub, 64 - 3 * row_tiles), jnp.bfloat16)], axis=2)
    got = lax.all_to_all(jnp.concatenate([body[:, 0], body[:, 1], first, tail], axis=2), "col", 0, 0)
    got = got.reshape(NB, -1)
    tags = got[:, 2 * quarter + eighth :].astype(jnp.float32)
    nug_own = tags[:, :3].T
    norm_bits = tags[:, 64 : 64 + 3 * row_tiles].reshape(NB, 3, row_tiles)
    norms = ((norm_bits[:, 0] + norm_bits[:, 1]) + norm_bits[:, 2]).T
    nug_sib = swap(nug_own)
    nug = jnp.concatenate([nug_own, nug_sib[1:]], axis=0).reshape(1, 5 * NB)

    up = [(i, (i + 1) % row_count) for i in range(row_count)]
    down = [(i, (i - 1) % row_count) for i in range(row_count)]
    homes = [lax.rem(row_index + 4 - d, row_count) for d in (0, 1, 3, 2)]

    zero_piece = got[:, 2 * quarter : 2 * quarter + eighth]
    below = lax.ppermute(zero_piece, "row", up)
    above = lax.ppermute(zero_piece, "row", down)
    far = jnp.concatenate(
        [lax.ppermute(below[: NB // 2], "row", up), lax.ppermute(above[NB // 2 :], "row", down)], axis=0)
    half0 = jnp.zeros((NB, 4 * eighth), jnp.bfloat16)
    for home, value in zip(homes, (zero_piece, below, above, far)):
        half0 = lax.dynamic_update_slice(half0, value, (0, home * eighth))
    half1 = swap(half0)
    even = jnp.where(core == 0, half0, half1).reshape(NB, 4, 1, eighth)
    odd = jnp.where(core == 0, half1, half0).reshape(NB, 4, 1, eighth)
    raw0 = jnp.concatenate([even, odd], axis=2).reshape(NB, features)
    wide0 = raw0.astype(jnp.float32)
    scaled0 = (wide0 * ard_weight).astype(jnp.bfloat16)
    norms0 = jnp.sum(wide0 * wide0 * ard_weight, axis=1)
    cross = lax.dot_general(raw0, scaled0, NT, preferred_element_type=jnp.float32)
    tile0 = jnp.exp(-0.5 * (norms0[:, None] + norms0[None, :] - 2.0 * cross)) + jnp.diag(nug[0, :NB])
    corner, inverse = factor_corner(0.5 * (tile0 + tile0.T))

    piece = got[:, : 2 * quarter].reshape(NB, 2, quarter).transpose(1, 0, 2)
    below = lax.ppermute(piece, "row", up)
    above = lax.ppermute(piece, "row", down)
    far = jnp.concatenate(
        [lax.ppermute(below[:1], "row", up), lax.ppermute(above[1:], "row", down)], axis=0)
    scaled_c = jnp.zeros((4, NB, features), jnp.bfloat16)
    norms_c = jnp.zeros((4, NB), jnp.float32)
    cross_c = jnp.zeros((4 * NB, NB), jnp.float32)
    for home, value in zip(homes, (piece, below, above, far)):
        raw = jnp.concatenate([value, swap(value)], axis=0)
        weight = lax.dynamic_slice_in_dim(ard_weight, home * quarter, quarter)
        wide = raw.astype(jnp.float32)
        scaled_c = lax.dynamic_update_slice(
            scaled_c, (wide * weight).astype(jnp.bfloat16), (0, 0, home * quarter))
        norms_c = norms_c + jnp.sum(wide * wide * weight, axis=2)
        against = lax.dynamic_slice_in_dim(scaled0, home * quarter, quarter, 1)
        cross_c = cross_c + lax.dot_general(
            raw.reshape(4 * NB, quarter), against, NT, preferred_element_type=jnp.float32)
    norms_c = norms_c.reshape(-1)
    kern_c = jnp.exp(-0.5 * (norms_c[:, None] + norms0[None, :] - 2.0 * cross_c))
    q_panel = stacked(dot_high(inverse, kern_c, NT))
    inverse3 = stacked(inverse.T)

    norms = norms.reshape(row_tiles, 4, 4, 2, sub)
    norms = lax.dynamic_index_in_dim(norms, core, 3, keepdims=False)
    norms = rolled(rolled(norms, 1, chip_y), 2, chip_x)
    ring_of = jnp.array(RING, jnp.int32)
    ys = lax.rem(chip_y + ring_of, 4)
    xs = lax.rem(chip_x + ring_of, 4)
    chips = ys[:, None] * 4 + xs[None, :]
    grow = (lax.iota(jnp.int32, row_tiles)[:, None, None, None] * row_count + row_index) * NB
    grow = grow + chips[None, :, :, None] * 16 + core * 8 + lax.iota(jnp.int32, sub)

    def arrange(value, order):
        a = value[:fold].transpose(1, 2, 0, 3).reshape(4, NB)
        b = value[fold:].transpose(2, 1, 0, 3).reshape(4, NB)
        return jnp.concatenate([a[order], b[order]]).reshape(-1, 1)

    near, last = slice(0, 3), slice(3, 4)

    def where_of(order):
        head = jnp.stack([row_index, col_index])
        lines = jnp.concatenate([chips[order], chips.T[order]]).reshape(-1)
        return jnp.concatenate([head, lines]).astype(jnp.int32)

    tile_j = jnp.stack([0 * col_index, col_index, col_index + 32, col_index ^ 1, (col_index ^ 1) + 32])
    gcol = (tile_j[:, None] * NB + lax.iota(jnp.int32, NB)).astype(jnp.int32).reshape(1, 5 * NB)
    wn = jnp.concatenate([norms0, norms_c]).reshape(1, -1)
    rest = (scaled0, scaled_c, wn, nug, gcol, inverse3, q_panel, corner)

    def flat(value):
        return value.reshape(-1, features)

    near_pieces = [flat(v) for v in (four_a, grid_a[0], grid_a[1], four_b, grid_b[0], grid_b[1])]
    near_cuts = tuple((i, 0, NB) for i in range(6))
    own1, sib1 = run_main(
        near_pieces, near_cuts, 3, where_of(near), arrange(norms, near), arrange(grow, near), rest)
    last_pieces = [flat(v) for v in (grid_a[2], grid_a[3], grid_b[2], grid_b[3])]
    last_cuts = ((0, 0, 128), (0, 128, 128), (1, 0, 128), (1, 128, 128))
    own2, sib2 = run_main(
        last_pieces, last_cuts, 1, where_of(last), arrange(norms, last), arrange(grow, last), rest)
    shape = (row_tiles, 16, 2, 4 * sub, 128)
    kinds1 = tuple((i < 3, i) for i in range(6))
    kinds2 = tuple((i < 1, i) for i in range(2))

    def lines(value):
        return value.reshape(-1, 4, fold, 4 * sub, 128)

    out = place((lines(own1), lines(swap(sib1))), ((True, kinds1), (False, kinds1)), where_of(near), None, shape)
    out = place((lines(own2), lines(swap(sib2))), ((True, kinds2), (False, kinds2)), where_of(last), out, shape)
    return out.reshape(row_tiles, 1, NB, 2, 1, NB)


def solution(mesh):
    placed = (P(None, "row", "col", None, None), P(), P(None, "row", "col", None))
    return jax.shard_map(
        local,
        mesh=mesh,
        in_specs=placed,
        out_specs=P(None, "row", None, None, "col", None),
        check_vma=False,
    )
```

```python
import functools

import jax
import jax.numpy as jnp
from jax import lax
from jax.experimental import pallas as pl
from jax.experimental.pallas import tpu as pltpu
from jax.sharding import PartitionSpec as P

NB = 256
HIGH = lax.Precision.HIGHEST
NT = (((1,), (1,)), ((), ()))
NN = (((1,), (0,)), ((), ()))
GRANT = 62 * 2**20
SMALL = pl.CostEstimate(flops=1, bytes_accessed=1, transcendentals=0)
VMEM = pl.BlockSpec(memory_space=pltpu.VMEM)
HBM = pl.BlockSpec(memory_space=pl.ANY)
SMEM = pl.BlockSpec(memory_space=pltpu.SMEM)


def dot_high(left, right, dims=NN):
    return lax.dot_general(left, right, dims, precision=HIGH, preferred_element_type=jnp.float32)


def dot_fast(left, right, dims):
    return lax.dot_general(left, right, dims, preferred_element_type=jnp.float32)


def halves(value):
    high = value.astype(jnp.bfloat16)
    low = (value - high.astype(jnp.float32)).astype(jnp.bfloat16)
    return high, low


def as_row(column):
    return jnp.broadcast_to(column, (column.shape[0], 128)).T[0:1, :]


def eliminate(block):
    size = block.shape[0]
    height = 32
    rows = lax.broadcasted_iota(jnp.int32, (size, size), 0)
    cols = lax.broadcasted_iota(jnp.int32, (size, size), 1)
    eye = (rows == cols).astype(jnp.float32)
    whole = jnp.concatenate([block, eye], axis=1)
    parts = [whole[g * height : (g + 1) * height] for g in range(size // height)]
    inner = lax.broadcasted_iota(jnp.int32, (height, 1), 0)
    for j in range(size):
        first, at = divmod(j, height)
        pivot_row = parts[first][at : at + 1, :]
        pivot_row = pivot_row * (1.0 / pivot_row[:, j : j + 1])
        for g in range(first, size // height):
            factor = parts[g][:, j : j + 1]
            if g == first:
                factor = jnp.where(inner > at, factor, 0.0)
            parts[g] = parts[g] - factor * pivot_row
    whole = jnp.concatenate(parts, axis=0)
    pivots = jnp.sum(whole[:, :size] * eye, axis=1, keepdims=True)
    root = lax.rsqrt(pivots)
    root = root * (1.5 - 0.5 * pivots * root * root)
    return whole[:, size:] * root


def store_factor(a_ref, l_ref, x_ref):
    half = NB // 2
    rows = lax.broadcasted_iota(jnp.int32, (half, half), 0)
    cols = lax.broadcasted_iota(jnp.int32, (half, half), 1)
    lower = rows >= cols
    zero = jnp.zeros((half, half), jnp.float32)
    a11, a21, a22 = a_ref[:half, :half], a_ref[half:, :half], a_ref[half:, half:]
    x11 = eliminate(a11)
    l21 = dot_high(a21, x11, NT)
    l_ref[:half, :half] = jnp.where(lower, dot_high(a11, x11, NT), 0.0)
    l_ref[:half, half:] = zero
    l_ref[half:, :half] = l21
    s22 = a22 - dot_high(l21, l21, NT)
    x22 = eliminate(s22)
    l_ref[half:, half:] = jnp.where(lower, dot_high(s22, x22, NT), 0.0)
    x_ref[:half, :half] = x11
    x_ref[:half, half:] = zero
    x_ref[half:, :half] = -dot_high(x22, dot_high(l21, x11))
    x_ref[half:, half:] = x22


def store_triple(out_ref, value):
    high, low = halves(value)
    size = value.shape[0]
    out_ref[:size, :] = high
    out_ref[size : 2 * size, :] = low
    out_ref[2 * size :, :] = high


def spots(where_ref, quarter):
    row = where_ref[0]
    return [pl.multiple_of(lax.rem(row + 4 - d, 4) * quarter, quarter) for d in (0, 1, 3, 2)]


def bring(sem, pairs):
    copies = [pltpu.make_async_copy(source, target, sem.at[n]) for n, (source, target) in enumerate(pairs)]
    for copy in copies:
        copy.start()
    for copy in copies:
        copy.wait()


def corner_kernel(where_ref, own_ref, below_ref, above_ref, far0_ref, far1_ref, weight_ref, nug_ref,
                  scaled_ref, norm_ref, l_ref, x_ref, x3_ref, raw_ref, a_ref, sem):
    quarter = own_ref.shape[1]
    own, below, above, far = spots(where_ref, quarter)
    bring(sem, (
        (own_ref, raw_ref.at[:, pl.ds(own, quarter)]),
        (below_ref, raw_ref.at[:, pl.ds(below, quarter)]),
        (above_ref, raw_ref.at[:, pl.ds(above, quarter)]),
        (far0_ref, raw_ref.at[: NB // 2, pl.ds(far, quarter)]),
        (far1_ref, raw_ref.at[NB // 2 :, pl.ds(far, quarter)]),
    ))
    norms = jnp.zeros((NB, 1), jnp.float32)
    cross = jnp.zeros((NB, NB), jnp.float32)
    for j in range(4):
        part = slice(j * quarter, (j + 1) * quarter)
        raw = raw_ref[:, part]
        wide = raw.astype(jnp.float32)
        product = wide * weight_ref[:, part]
        scaled = product.astype(jnp.bfloat16)
        scaled_ref[:, part] = scaled
        norms += jnp.sum(wide * wide * weight_ref[:, part], axis=1, keepdims=True)
        cross += dot_fast(raw, scaled, NT)
    row_norms = as_row(norms)
    norm_ref[...] = row_norms
    eye = lax.broadcasted_iota(jnp.int32, (NB, NB), 0) == lax.broadcasted_iota(jnp.int32, (NB, NB), 1)
    tile = jnp.exp(-0.5 * (norms + row_norms - 2.0 * cross)) + jnp.where(eye, nug_ref[...], 0.0)
    a_ref[...] = 0.5 * (tile + tile.T)
    store_factor(a_ref, l_ref, x_ref)
    store_triple(x3_ref, x_ref[...].T)


def column_kernel(where_ref, own_ref, below_ref, above_ref, far0_ref, far1_ref, weight_ref, scaled0_ref, norm0_ref,
                  x_ref, scaled_ref, norm_ref, q_ref, raw_ref, zero_ref, sem):
    quarter = own_ref.shape[1] // 2
    own, below, above, far = spots(where_ref, quarter)
    pairs = [(scaled0_ref, zero_ref)]
    for u in range(2):
        rows = slice(u * NB, (u + 1) * NB)
        part = slice(u * quarter, (u + 1) * quarter)
        pairs += [
            (own_ref.at[:, part], raw_ref.at[rows, pl.ds(own, quarter)]),
            (below_ref.at[:, part], raw_ref.at[rows, pl.ds(below, quarter)]),
            (above_ref.at[:, part], raw_ref.at[rows, pl.ds(above, quarter)]),
            (far0_ref.at[:, part], raw_ref.at[u * NB : u * NB + NB // 2, pl.ds(far, quarter)]),
            (far1_ref.at[:, part], raw_ref.at[u * NB + NB // 2 : (u + 1) * NB, pl.ds(far, quarter)]),
        ]
    bring(sem, pairs)
    norms = jnp.zeros((2 * NB, 1), jnp.float32)
    cross = jnp.zeros((2 * NB, NB), jnp.float32)
    for j in range(4):
        part = slice(j * quarter, (j + 1) * quarter)
        raw = raw_ref[:, part]
        wide = raw.astype(jnp.float32)
        scaled_ref[:, part] = (wide * weight_ref[:, part]).astype(jnp.bfloat16)
        norms += jnp.sum(wide * wide * weight_ref[:, part], axis=1, keepdims=True)
        cross += dot_fast(raw, zero_ref[:, part], NT)
    norm_ref[...] = as_row(norms)
    kern = jnp.exp(-0.5 * (norms + norm0_ref[...] - 2.0 * cross))
    store_triple(q_ref, dot_high(x_ref[...], kern, NT))


def main_kernel(tiles, rows_dev, where_ref, rows_ref, norm_ref, w0_ref, wc_ref, wn_ref, nug_ref, inv_ref, q_ref, l_ref, o_ref):
    step = pl.program_id(0)
    row, col = where_ref[0], where_ref[1]
    eye = lax.broadcasted_iota(jnp.int32, (NB, NB), 0) == lax.broadcasted_iota(jnp.int32, (NB, NB), 1)
    for n in range(tiles):
        tile = (step * tiles + n) * rows_dev + row
        data = rows_ref[n * NB : (n + 1) * NB, :]
        cross = jnp.concatenate([dot_fast(data, w0_ref[...], NT), dot_fast(data, wc_ref[...], NT)], axis=1)
        norms = norm_ref[n * NB : (n + 1) * NB, :]
        kern = jnp.exp(-0.5 * (norms + wn_ref[...] - 2.0 * cross))
        left = kern[:, :NB] + jnp.where(eye & (tile == 0), nug_ref[:, :NB], 0.0)
        high, low = halves(left)
        panel = lax.dot_general(
            jnp.concatenate([high, high, low], axis=1), inv_ref[...], NN, preferred_element_type=jnp.float32
        )
        high, low = halves(panel)
        update = lax.dot_general(
            jnp.concatenate([high, high, low], axis=1), q_ref[...], NN, preferred_element_type=jnp.float32
        )
        first_tile = tile == 0
        for u in range(2):
            part = slice(NB * (u + 1), NB * (u + 2))
            own = kern[:, part] + jnp.where(eye & (tile == col + 32 * u), nug_ref[:, part], 0.0)
            result = jnp.where(first_tile, own, own - update[:, NB * u : NB * (u + 1)])
            if u == 0:
                result = jnp.where(col == 0, jnp.where(first_tile, l_ref[...], panel), result)
            for half in range(2):
                o_ref[pl.ds(n * NB * 4 + 2 * u + half, NB, stride=4), :] = result[:, 128 * half : 128 * (half + 1)]


def local(samples, ard_weight, nugget):
    row_count = lax.axis_size("row")
    col_count = lax.axis_size("col")
    row_index = lax.axis_index("row")
    col_index = lax.axis_index("col")
    row_tiles, _, _, sub, features = samples.shape
    quarter = features // row_count
    fold = row_tiles // 2
    own = samples.reshape(row_tiles, sub, features)
    weight_row = ard_weight.reshape(1, features)
    f32, bf16 = jnp.float32, jnp.bfloat16
    shape = jax.ShapeDtypeStruct

    gathered = lax.all_gather(samples, "col", axis=2, tiled=True)

    widened = own.astype(f32)
    own_norms = jnp.sum(widened * widened * ard_weight, axis=2)
    n_high = lax.reduce_precision(own_norms, 8, 7)
    n_mid = lax.reduce_precision(own_norms - n_high, 8, 7)
    n_low = own_norms - n_high - n_mid
    bits = jnp.stack([n_high, n_mid, n_low]).astype(bf16).transpose(2, 0, 1).reshape(sub, 3 * row_tiles)

    cut = own.reshape(row_tiles, sub, row_count, quarter).transpose(2, 0, 1, 3)
    extra = jnp.broadcast_to(nugget.reshape(1, row_tiles, sub, 1), (row_count, row_tiles, sub, 128))
    sent = lax.all_to_all(jnp.concatenate([cut, extra], axis=3), "row", 0, 0)
    sent = sent.reshape(row_count, 2, fold, sub, quarter + 128).transpose(2, 0, 1, 3, 4)
    sent = sent.reshape(col_count, 2, sub, quarter + 128)
    body = sent[..., :quarter]
    tags = sent[..., quarter]
    tail = jnp.concatenate(
        [jnp.broadcast_to(tags[0, 0][None, :, None], (col_count, sub, 1)),
         tags[:, 0, :, None], tags[:, 1, :, None],
         jnp.zeros((col_count, sub, 61), bf16),
         jnp.broadcast_to(bits[None], (col_count, sub, 3 * row_tiles)),
         jnp.zeros((col_count, sub, 64 - 3 * row_tiles), bf16)], axis=2)
    first = jnp.broadcast_to(body[0, 0][None], (col_count, sub, quarter))
    got = lax.all_to_all(jnp.concatenate([body[:, 0], body[:, 1], first, tail], axis=2), "col", 0, 0)
    got = got.reshape(NB, -1)
    tags = got[:, 3 * quarter :].astype(f32)
    nug = tags[:, :3].T.reshape(1, 3 * NB)
    norm_bits = tags[:, 64 : 64 + 3 * row_tiles].reshape(NB, 3, row_tiles)
    norms = ((norm_bits[:, 0] + norm_bits[:, 1]) + norm_bits[:, 2]).T

    up = [(i, (i + 1) % row_count) for i in range(row_count)]
    down = [(i, (i - 1) % row_count) for i in range(row_count)]

    where = jnp.stack([row_index, col_index]).astype(jnp.int32)
    norms = norms.reshape(-1, 1)

    zero = got[:, 2 * quarter : 3 * quarter]
    below0, above0 = lax.ppermute(zero, "row", up), lax.ppermute(zero, "row", down)
    zero_far = (below0, above0, lax.ppermute(below0[: NB // 2], "row", up),
                lax.ppermute(above0[NB // 2 :], "row", down))
    zero_far, got = lax.optimization_barrier((zero_far, got))
    cols = got[:, : 2 * quarter]
    below, above = lax.ppermute(cols, "row", up), lax.ppermute(cols, "row", down)
    scaled0, norms0, corner, inverse, inverse3 = pl.pallas_call(
        corner_kernel,
        out_shape=(shape((NB, features), bf16), shape((1, NB), f32), shape((NB, NB), f32), shape((NB, NB), f32),
                   shape((3 * NB, NB), bf16)),
        in_specs=[SMEM] + [HBM] * 5 + [VMEM] * 2,
        out_specs=(VMEM,) * 5,
        scratch_shapes=[pltpu.VMEM((NB, features), bf16), pltpu.VMEM((NB, NB), f32), pltpu.SemaphoreType.DMA((5,))],
        cost_estimate=SMALL,
        compiler_params=pltpu.CompilerParams(vmem_limit_bytes=GRANT),
    )(where, zero, *zero_far, weight_row, nug[:, :NB])
    corner, below, above = lax.optimization_barrier((corner, below, above))
    cols_far = (below, above, lax.ppermute(below[: NB // 2], "row", up), lax.ppermute(above[NB // 2 :], "row", down))
    scaled, norms_c, q_panel = pl.pallas_call(
        column_kernel,
        out_shape=(shape((2 * NB, features), bf16), shape((1, 2 * NB), f32), shape((3 * NB, 2 * NB), bf16)),
        in_specs=[SMEM] + [HBM] * 5 + [VMEM, HBM] + [VMEM] * 2,
        out_specs=(VMEM,) * 3,
        scratch_shapes=[pltpu.VMEM((2 * NB, features), bf16), pltpu.VMEM((NB, features), bf16),
                        pltpu.SemaphoreType.DMA((11,))],
        cost_estimate=SMALL,
        compiler_params=pltpu.CompilerParams(vmem_limit_bytes=GRANT),
    )(where, cols, *cols_far, weight_row, scaled0, norms0, inverse)

    fixed = (scaled0, scaled, jnp.concatenate([norms0, norms_c], axis=1), nug, inverse3, q_panel, corner)

    def whole(value):
        return pl.BlockSpec(value.shape, lambda i, _: (0, 0), pipeline_mode=pl.Buffered(1))

    rows_data = gathered.reshape(row_tiles * NB, features)
    tiles = 2
    out = pl.pallas_call(
        functools.partial(main_kernel, tiles, 4),
        out_shape=shape((row_tiles * NB * 4, 128), f32),
        grid_spec=pltpu.PrefetchScalarGridSpec(
            num_scalar_prefetch=1,
            grid=(row_tiles // tiles,),
            in_specs=[
                pl.BlockSpec((tiles * NB, features), lambda i, _: (i, 0)),
                pl.BlockSpec((tiles * NB, 1), lambda i, _: (i, 0)),
            ] + [whole(v) for v in fixed],
            out_specs=pl.BlockSpec((tiles * NB * 4, 128), lambda i, _: (i, 0)),
        ),
        compiler_params=pltpu.CompilerParams(vmem_limit_bytes=GRANT),
        cost_estimate=pl.CostEstimate(flops=30 * 10**9, bytes_accessed=48 * 2**20, transcendentals=0),
    )(where, rows_data, norms, *fixed)
    return out.reshape(row_tiles, 1, NB, 2, 1, NB)


def solution(mesh):
    placed = (P(None, "row", "col", None, None), P(), P(None, "row", "col", None))
    return jax.shard_map(
        local,
        mesh=mesh,
        in_specs=placed,
        out_specs=P(None, "row", None, None, "col", None),
        check_vma=False,
    )
```

```python
import functools

import jax
import jax.numpy as jnp
from jax import lax
from jax.experimental import pallas as pl
from jax.experimental.pallas import tpu as pltpu
from jax.sharding import PartitionSpec as P

NB = 256
HIGH = lax.Precision.HIGHEST
NT = (((1,), (1,)), ((), ()))
NN = (((1,), (0,)), ((), ()))
RING = (0, 3, 1, 2)
GRANT = 62 * 2**20
SMALL = pl.CostEstimate(flops=1, bytes_accessed=1, transcendentals=0)
VMEM = pl.BlockSpec(memory_space=pltpu.VMEM)
HBM = pl.BlockSpec(memory_space=pl.ANY)
SMEM = pl.BlockSpec(memory_space=pltpu.SMEM)


def dot_high(left, right, dims=NN):
    return lax.dot_general(left, right, dims, precision=HIGH, preferred_element_type=jnp.float32)


def dot_fast(left, right, dims):
    return lax.dot_general(left, right, dims, preferred_element_type=jnp.float32)


def halves(value):
    high = value.astype(jnp.bfloat16)
    low = (value - high.astype(jnp.float32)).astype(jnp.bfloat16)
    return high, low


def as_row(column):
    return jnp.broadcast_to(column, (column.shape[0], 128)).T[0:1, :]


def eliminate(block):
    size = block.shape[0]
    height = 32
    rows = lax.broadcasted_iota(jnp.int32, (size, size), 0)
    cols = lax.broadcasted_iota(jnp.int32, (size, size), 1)
    eye = (rows == cols).astype(jnp.float32)
    whole = jnp.concatenate([block, eye], axis=1)
    parts = [whole[g * height : (g + 1) * height] for g in range(size // height)]
    inner = lax.broadcasted_iota(jnp.int32, (height, 1), 0)
    for j in range(size):
        first, at = divmod(j, height)
        pivot_row = parts[first][at : at + 1, :]
        pivot_row = pivot_row * (1.0 / pivot_row[:, j : j + 1])
        for g in range(first, size // height):
            factor = parts[g][:, j : j + 1]
            if g == first:
                factor = jnp.where(inner > at, factor, 0.0)
            parts[g] = parts[g] - factor * pivot_row
    whole = jnp.concatenate(parts, axis=0)
    pivots = jnp.sum(whole[:, :size] * eye, axis=1, keepdims=True)
    root = lax.rsqrt(pivots)
    root = root * (1.5 - 0.5 * pivots * root * root)
    return whole[:, size:] * root


def store_factor(a_ref, l_ref, x_ref):
    half = NB // 2
    rows = lax.broadcasted_iota(jnp.int32, (half, half), 0)
    cols = lax.broadcasted_iota(jnp.int32, (half, half), 1)
    lower = rows >= cols
    zero = jnp.zeros((half, half), jnp.float32)
    a11, a21, a22 = a_ref[:half, :half], a_ref[half:, :half], a_ref[half:, half:]
    x11 = eliminate(a11)
    l21 = dot_high(a21, x11, NT)
    l_ref[:half, :half] = jnp.where(lower, dot_high(a11, x11, NT), 0.0)
    l_ref[:half, half:] = zero
    l_ref[half:, :half] = l21
    s22 = a22 - dot_high(l21, l21, NT)
    x22 = eliminate(s22)
    l_ref[half:, half:] = jnp.where(lower, dot_high(s22, x22, NT), 0.0)
    x_ref[:half, :half] = x11
    x_ref[:half, half:] = zero
    x_ref[half:, :half] = -dot_high(x22, dot_high(l21, x11))
    x_ref[half:, half:] = x22


def store_triple(out_ref, value):
    high, low = halves(value)
    size = value.shape[0]
    out_ref[:size, :] = high
    out_ref[size : 2 * size, :] = low
    out_ref[2 * size :, :] = high


def spots(where_ref, quarter):
    row = where_ref[0]
    return [pl.multiple_of(lax.rem(row + 4 - d, 4) * quarter, quarter) for d in (0, 1, 3, 2)]


def bring(sem, pairs):
    copies = [pltpu.make_async_copy(source, target, sem.at[n]) for n, (source, target) in enumerate(pairs)]
    for copy in copies:
        copy.start()
    for copy in copies:
        copy.wait()


def corner_kernel(where_ref, mine_ref, theirs_ref, weight_ref, nug_ref,
                  scaled_ref, norm_ref, l_ref, x_ref, x3_ref, raw_ref, a_ref, sem):
    lines, half = mine_ref.shape[1:]
    quarter = half // 2
    core = lax.rem(where_ref[1], 2)
    pairs = []
    for n in range(mine_ref.shape[0]):
        rows = pl.ds(pl.multiple_of(where_ref[2 + n] * lines, lines), lines)
        pairs.append((mine_ref.at[n], raw_ref.at[rows, pl.ds(pl.multiple_of(core * half, half), half)]))
        pairs.append((theirs_ref.at[n], raw_ref.at[rows, pl.ds(pl.multiple_of((1 - core) * half, half), half)]))
    bring(sem, pairs)
    norms = jnp.zeros((NB, 1), jnp.float32)
    cross = jnp.zeros((NB, NB), jnp.float32)
    for j in range(4):
        part = slice(j * quarter, (j + 1) * quarter)
        raw = raw_ref[:, part]
        wide = raw.astype(jnp.float32)
        product = wide * weight_ref[:, part]
        scaled = product.astype(jnp.bfloat16)
        scaled_ref[:, part] = scaled
        norms += jnp.sum(wide * wide * weight_ref[:, part], axis=1, keepdims=True)
        cross += dot_fast(raw, scaled, NT)
    row_norms = as_row(norms)
    norm_ref[...] = row_norms
    eye = lax.broadcasted_iota(jnp.int32, (NB, NB), 0) == lax.broadcasted_iota(jnp.int32, (NB, NB), 1)
    tile = jnp.exp(-0.5 * (norms + row_norms - 2.0 * cross)) + jnp.where(eye, nug_ref[...], 0.0)
    a_ref[...] = 0.5 * (tile + tile.T)
    store_factor(a_ref, l_ref, x_ref)
    store_triple(x3_ref, x_ref[...].T)


def column_kernel(where_ref, own_ref, below_ref, above_ref, far0_ref, far1_ref, weight_ref, scaled0_ref, norm0_ref,
                  x_ref, scaled_ref, norm_ref, q_ref, raw_ref, zero_ref, sem):
    quarter = own_ref.shape[1] // 2
    own, below, above, far = spots(where_ref, quarter)
    pairs = [(scaled0_ref, zero_ref)]
    for u in range(2):
        rows = slice(u * NB, (u + 1) * NB)
        part = slice(u * quarter, (u + 1) * quarter)
        pairs += [
            (own_ref.at[:, part], raw_ref.at[rows, pl.ds(own, quarter)]),
            (below_ref.at[:, part], raw_ref.at[rows, pl.ds(below, quarter)]),
            (above_ref.at[:, part], raw_ref.at[rows, pl.ds(above, quarter)]),
            (far0_ref.at[:, part], raw_ref.at[u * NB : u * NB + NB // 2, pl.ds(far, quarter)]),
            (far1_ref.at[:, part], raw_ref.at[u * NB + NB // 2 : (u + 1) * NB, pl.ds(far, quarter)]),
        ]
    bring(sem, pairs)
    norms = jnp.zeros((2 * NB, 1), jnp.float32)
    cross = jnp.zeros((2 * NB, NB), jnp.float32)
    for j in range(4):
        part = slice(j * quarter, (j + 1) * quarter)
        raw = raw_ref[:, part]
        wide = raw.astype(jnp.float32)
        scaled_ref[:, part] = (wide * weight_ref[:, part]).astype(jnp.bfloat16)
        norms += jnp.sum(wide * wide * weight_ref[:, part], axis=1, keepdims=True)
        cross += dot_fast(raw, zero_ref[:, part], NT)
    norm_ref[...] = as_row(norms)
    kern = jnp.exp(-0.5 * (norms + norm0_ref[...] - 2.0 * cross))
    store_triple(q_ref, dot_high(x_ref[...], kern, NT))


def main_kernel(tiles, rows_dev, where_ref, rows_ref, norm_ref, w0_ref, wc_ref, wn_ref, nug_ref, inv_ref, q_ref, l_ref, o_ref):
    step = pl.program_id(0)
    row, col = where_ref[0], where_ref[1]
    eye = lax.broadcasted_iota(jnp.int32, (NB, NB), 0) == lax.broadcasted_iota(jnp.int32, (NB, NB), 1)
    for n in range(tiles):
        tile = (step * tiles + n) * rows_dev + row
        data = rows_ref[n * NB : (n + 1) * NB, :]
        cross = jnp.concatenate([dot_fast(data, w0_ref[...], NT), dot_fast(data, wc_ref[...], NT)], axis=1)
        norms = norm_ref[n * NB : (n + 1) * NB, :]
        kern = jnp.exp(-0.5 * (norms + wn_ref[...] - 2.0 * cross))
        left = kern[:, :NB] + jnp.where(eye & (tile == 0), nug_ref[:, :NB], 0.0)
        high, low = halves(left)
        panel = lax.dot_general(
            jnp.concatenate([high, high, low], axis=1), inv_ref[...], NN, preferred_element_type=jnp.float32
        )
        high, low = halves(panel)
        update = lax.dot_general(
            jnp.concatenate([high, high, low], axis=1), q_ref[...], NN, preferred_element_type=jnp.float32
        )
        first_tile = tile == 0
        for u in range(2):
            part = slice(NB * (u + 1), NB * (u + 2))
            own = kern[:, part] + jnp.where(eye & (tile == col + 32 * u), nug_ref[:, part], 0.0)
            result = jnp.where(first_tile, own, own - update[:, NB * u : NB * (u + 1)])
            if u == 0:
                result = jnp.where(col == 0, jnp.where(first_tile, l_ref[...], panel), result)
            for half in range(2):
                o_ref[pl.ds(n * NB * 4 + 2 * u + half, NB, stride=4), :] = result[:, 128 * half : 128 * (half + 1)]


def x_move(step):
    return [(y * 8 + x * 2 + k, y * 8 + (x + step) % 4 * 2 + k) for y in range(4) for x in range(4) for k in range(2)]


def y_move(step):
    return [(y * 8 + x * 2 + k, (y + step) % 4 * 8 + x * 2 + k) for y in range(4) for x in range(4) for k in range(2)]


def ring_join(value, moves):
    return jnp.concatenate([value] + [lax.ppermute(value, "col", moves(step)) for step in (1, -1, 2)], axis=0)


def local(samples, ard_weight, nugget):
    row_count = lax.axis_size("row")
    col_count = lax.axis_size("col")
    row_index = lax.axis_index("row")
    col_index = lax.axis_index("col")
    row_tiles, _, _, sub, features = samples.shape
    quarter = features // row_count
    fold = row_tiles // 2
    own = samples.reshape(row_tiles, sub, features)
    weight_row = ard_weight.reshape(1, features)
    f32, bf16 = jnp.float32, jnp.bfloat16
    shape = jax.ShapeDtypeStruct

    gathered = lax.all_gather(samples, "col", axis=2, tiled=True)

    widened = own.astype(f32)
    own_norms = jnp.sum(widened * widened * ard_weight, axis=2)
    n_high = lax.reduce_precision(own_norms, 8, 7)
    n_mid = lax.reduce_precision(own_norms - n_high, 8, 7)
    n_low = own_norms - n_high - n_mid
    bits = jnp.stack([n_high, n_mid, n_low]).astype(bf16).transpose(2, 0, 1).reshape(sub, 3 * row_tiles)

    cut = own.reshape(row_tiles, sub, row_count, quarter).transpose(2, 0, 1, 3)
    extra = jnp.broadcast_to(nugget.reshape(1, row_tiles, sub, 1), (row_count, row_tiles, sub, 128))
    share = features // row_tiles
    zero = own[0].reshape(sub, row_tiles, share).transpose(1, 0, 2)
    zero = jnp.broadcast_to(zero[None], (row_count, row_tiles, sub, share))
    sent = lax.all_to_all(jnp.concatenate([cut, extra, zero], axis=3), "row", 0, 0)
    zero = sent[0, :, :, quarter + 128 :].transpose(1, 0, 2).reshape(sub, features)
    sent = sent[..., : quarter + 128].reshape(row_count, 2, fold, sub, quarter + 128).transpose(2, 0, 1, 3, 4)
    sent = sent.reshape(col_count, 2, sub, quarter + 128)

    core = col_index % 2
    chip_x, chip_y = col_index // 2 % 4, col_index // 8
    sibling = [(i, i ^ 1) for i in range(col_count)]
    left, right = zero[:, : features // 2], zero[:, features // 2 :]
    kept = jnp.where(core == 0, left, right)
    came = lax.ppermute(jnp.where(core == 0, right, left), "col", sibling)
    block = jnp.where(core == 0, jnp.concatenate([kept, came]), jnp.concatenate([came, kept]))
    mine = ring_join(ring_join(block[None], x_move), y_move)
    theirs = lax.ppermute(mine, "col", sibling)
    body = sent[..., :quarter]
    tags = sent[..., quarter]
    tail = jnp.concatenate(
        [jnp.broadcast_to(tags[0, 0][None, :, None], (col_count, sub, 1)),
         tags[:, 0, :, None], tags[:, 1, :, None],
         jnp.zeros((col_count, sub, 61), bf16),
         jnp.broadcast_to(bits[None], (col_count, sub, 3 * row_tiles)),
         jnp.zeros((col_count, sub, 64 - 3 * row_tiles), bf16)], axis=2)
    got = lax.all_to_all(jnp.concatenate([body[:, 0], body[:, 1], tail], axis=2), "col", 0, 0)
    got = got.reshape(NB, -1)
    tags = got[:, 2 * quarter :].astype(f32)
    nug = tags[:, :3].T.reshape(1, 3 * NB)
    norm_bits = tags[:, 64 : 64 + 3 * row_tiles].reshape(NB, 3, row_tiles)
    norms = ((norm_bits[:, 0] + norm_bits[:, 1]) + norm_bits[:, 2]).T

    up = [(i, (i + 1) % row_count) for i in range(row_count)]
    down = [(i, (i - 1) % row_count) for i in range(row_count)]

    ring_of = jnp.array(RING, jnp.int32)
    chips = lax.rem(chip_y + ring_of, 4)[:, None] * 4 + lax.rem(chip_x + ring_of, 4)[None, :]
    where = jnp.concatenate([jnp.stack([row_index, col_index]), chips.reshape(-1)]).astype(jnp.int32)
    norms = norms.reshape(-1, 1)

    cols = got[:, : 2 * quarter]
    below, above = lax.ppermute(cols, "row", up), lax.ppermute(cols, "row", down)
    scaled0, norms0, corner, inverse, inverse3 = pl.pallas_call(
        corner_kernel,
        out_shape=(shape((NB, features), bf16), shape((1, NB), f32), shape((NB, NB), f32), shape((NB, NB), f32),
                   shape((3 * NB, NB), bf16)),
        in_specs=[SMEM] + [HBM] * 2 + [VMEM] * 2,
        out_specs=(VMEM,) * 5,
        scratch_shapes=[pltpu.VMEM((NB, features), bf16), pltpu.VMEM((NB, NB), f32), pltpu.SemaphoreType.DMA((32,))],
        cost_estimate=SMALL,
        compiler_params=pltpu.CompilerParams(vmem_limit_bytes=GRANT),
    )(where, mine, theirs, weight_row, nug[:, :NB])
    corner, below, above = lax.optimization_barrier((corner, below, above))
    cols_far = (below, above, lax.ppermute(below[: NB // 2], "row", up), lax.ppermute(above[NB // 2 :], "row", down))
    scaled, norms_c, q_panel = pl.pallas_call(
        column_kernel,
        out_shape=(shape((2 * NB, features), bf16), shape((1, 2 * NB), f32), shape((3 * NB, 2 * NB), bf16)),
        in_specs=[SMEM] + [HBM] * 5 + [VMEM, HBM] + [VMEM] * 2,
        out_specs=(VMEM,) * 3,
        scratch_shapes=[pltpu.VMEM((2 * NB, features), bf16), pltpu.VMEM((NB, features), bf16),
                        pltpu.SemaphoreType.DMA((11,))],
        cost_estimate=SMALL,
        compiler_params=pltpu.CompilerParams(vmem_limit_bytes=GRANT),
    )(where, cols, *cols_far, weight_row, scaled0, norms0, inverse)

    fixed = (scaled0, scaled, jnp.concatenate([norms0, norms_c], axis=1), nug, inverse3, q_panel, corner)

    def whole(value):
        return pl.BlockSpec(value.shape, lambda i, _: (0, 0), pipeline_mode=pl.Buffered(1))

    rows_data = gathered.reshape(row_tiles * NB, features)
    tiles = 2
    out = pl.pallas_call(
        functools.partial(main_kernel, tiles, 4),
        out_shape=shape((row_tiles * NB * 4, 128), f32),
        grid_spec=pltpu.PrefetchScalarGridSpec(
            num_scalar_prefetch=1,
            grid=(row_tiles // tiles,),
            in_specs=[
                pl.BlockSpec((tiles * NB, features), lambda i, _: (i, 0)),
                pl.BlockSpec((tiles * NB, 1), lambda i, _: (i, 0)),
            ] + [whole(v) for v in fixed],
            out_specs=pl.BlockSpec((tiles * NB * 4, 128), lambda i, _: (i, 0)),
        ),
        compiler_params=pltpu.CompilerParams(vmem_limit_bytes=GRANT),
        cost_estimate=pl.CostEstimate(flops=30 * 10**9, bytes_accessed=48 * 2**20, transcendentals=0),
    )(where, rows_data, norms, *fixed)
    return out.reshape(row_tiles, 1, NB, 2, 1, NB)


def solution(mesh):
    placed = (P(None, "row", "col", None, None), P(), P(None, "row", "col", None))
    return jax.shard_map(
        local,
        mesh=mesh,
        in_specs=placed,
        out_specs=P(None, "row", None, None, "col", None),
        check_vma=False,
    )
```

```python
import functools

import jax
import jax.numpy as jnp
from jax import lax
from jax.experimental import pallas as pl
from jax.experimental.pallas import tpu as pltpu
from jax.sharding import PartitionSpec as P

NB = 256
HIGH = lax.Precision.HIGHEST
NT = (((1,), (1,)), ((), ()))
NN = (((1,), (0,)), ((), ()))
RING = (0, 3, 1, 2)
GRANT = 62 * 2**20
SMALL = pl.CostEstimate(flops=1, bytes_accessed=1, transcendentals=0)
VMEM = pl.BlockSpec(memory_space=pltpu.VMEM)
HBM = pl.BlockSpec(memory_space=pl.ANY)
SMEM = pl.BlockSpec(memory_space=pltpu.SMEM)


def dot_high(left, right, dims=NN):
    return lax.dot_general(left, right, dims, precision=HIGH, preferred_element_type=jnp.float32)


def dot_fast(left, right, dims):
    return lax.dot_general(left, right, dims, preferred_element_type=jnp.float32)


def halves(value):
    high = value.astype(jnp.bfloat16)
    low = (value - high.astype(jnp.float32)).astype(jnp.bfloat16)
    return high, low


def as_row(column):
    return jnp.broadcast_to(column, (column.shape[0], 128)).T[0:1, :]


def eliminate(block):
    size = block.shape[0]
    height = 32
    rows = lax.broadcasted_iota(jnp.int32, (size, size), 0)
    cols = lax.broadcasted_iota(jnp.int32, (size, size), 1)
    parts = [block[g * height : (g + 1) * height] for g in range(size // height)]
    inner = lax.broadcasted_iota(jnp.int32, (height, 1), 0)
    lane = lax.broadcasted_iota(jnp.int32, (1, size), 1)

    def spread(value):
        return jnp.broadcast_to(value, (value.shape[0], size))

    for j in range(0, size, 2):
        first, at = divmod(j, height)
        row0 = parts[first][at : at + 1, :]
        row1 = parts[first][at + 1 : at + 2, :]
        a, b = spread(row0[:, j : j + 1]), spread(row0[:, j + 1 : j + 2])
        c, d = spread(row1[:, j : j + 1]), spread(row1[:, j + 1 : j + 2])
        inverse = 1.0 / a
        scale, ratio = c * inverse, b * inverse
        row0 = row0 + (lane == j).astype(jnp.float32)
        row1 = row1 - scale * row0 + (lane == j + 1).astype(jnp.float32)
        row1 = row1 * (1.0 / (d - scale * b))
        row0 = row0 * inverse
        for g in range(first, size // height):
            left = spread(parts[g][:, j : j + 1])
            right = spread(parts[g][:, j + 1 : j + 2]) - left * ratio
            if g == first:
                left = jnp.where(inner > at, left, 0.0)
                right = jnp.where(inner > at + 1, right, 0.0)
            parts[g] = parts[g] - left * row0 - right * row1
    whole = jnp.concatenate(parts, axis=0)
    eye = (rows == cols).astype(jnp.float32)
    pivots = jnp.sum(whole * eye, axis=1, keepdims=True)
    root = lax.rsqrt(pivots)
    root = root * (1.5 - 0.5 * pivots * root * root)
    return jnp.where(rows > cols, whole, eye) * root


def store_factor(a_ref, l_ref, x_ref):
    half = NB // 2
    rows = lax.broadcasted_iota(jnp.int32, (half, half), 0)
    cols = lax.broadcasted_iota(jnp.int32, (half, half), 1)
    lower = rows >= cols
    zero = jnp.zeros((half, half), jnp.float32)
    a11, a21, a22 = a_ref[:half, :half], a_ref[half:, :half], a_ref[half:, half:]
    x11 = eliminate(a11)
    l21 = dot_high(a21, x11, NT)
    l_ref[:half, :half] = jnp.where(lower, dot_high(a11, x11, NT), 0.0)
    l_ref[:half, half:] = zero
    l_ref[half:, :half] = l21
    s22 = a22 - dot_high(l21, l21, NT)
    x22 = eliminate(s22)
    l_ref[half:, half:] = jnp.where(lower, dot_high(s22, x22, NT), 0.0)
    x_ref[:half, :half] = x11
    x_ref[:half, half:] = zero
    x_ref[half:, :half] = -dot_high(x22, dot_high(l21, x11))
    x_ref[half:, half:] = x22


def store_triple(out_ref, value):
    high, low = halves(value)
    size = value.shape[0]
    out_ref[:size, :] = high
    out_ref[size : 2 * size, :] = low
    out_ref[2 * size :, :] = high


def spots(where_ref, quarter):
    row = where_ref[0]
    return [pl.multiple_of(lax.rem(row + 4 - d, 4) * quarter, quarter) for d in (0, 1, 3, 2)]


def bring(sem, pairs):
    copies = [pltpu.make_async_copy(source, target, sem.at[n]) for n, (source, target) in enumerate(pairs)]
    for copy in copies:
        copy.start()
    for copy in copies:
        copy.wait()


def corner_kernel(where_ref, mine_ref, theirs_ref, weight_ref, nug_ref,
                  scaled_ref, norm_ref, l_ref, x_ref, x3_ref, raw_ref, a_ref, sem):
    lines, half = mine_ref.shape[1:]
    quarter = half // 2
    core = lax.rem(where_ref[1], 2)
    pairs = []
    for n in range(mine_ref.shape[0]):
        rows = pl.ds(pl.multiple_of(where_ref[2 + n] * lines, lines), lines)
        pairs.append((mine_ref.at[n], raw_ref.at[rows, pl.ds(pl.multiple_of(core * half, half), half)]))
        pairs.append((theirs_ref.at[n], raw_ref.at[rows, pl.ds(pl.multiple_of((1 - core) * half, half), half)]))
    bring(sem, pairs)
    norms = jnp.zeros((NB, 1), jnp.float32)
    cross = jnp.zeros((NB, NB), jnp.float32)
    for j in range(4):
        part = slice(j * quarter, (j + 1) * quarter)
        raw = raw_ref[:, part]
        wide = raw.astype(jnp.float32)
        product = wide * weight_ref[:, part]
        scaled = product.astype(jnp.bfloat16)
        scaled_ref[:, part] = scaled
        norms += jnp.sum(wide * wide * weight_ref[:, part], axis=1, keepdims=True)
        cross += dot_fast(raw, scaled, NT)
    row_norms = as_row(norms)
    norm_ref[...] = row_norms
    eye = lax.broadcasted_iota(jnp.int32, (NB, NB), 0) == lax.broadcasted_iota(jnp.int32, (NB, NB), 1)
    tile = jnp.exp(-0.5 * (norms + row_norms - 2.0 * cross)) + jnp.where(eye, nug_ref[...], 0.0)
    a_ref[...] = 0.5 * (tile + tile.T)
    store_factor(a_ref, l_ref, x_ref)
    store_triple(x3_ref, x_ref[...].T)


def column_kernel(where_ref, own_ref, below_ref, above_ref, weight_ref, scaled0_ref,
                  scaled_ref, norm_ref, cross_ref, raw_ref, zero_ref, sem):
    quarter = own_ref.shape[1] // 2
    pairs = [(scaled0_ref, zero_ref)]
    for n, ref in enumerate((own_ref, below_ref, above_ref)):
        for u in range(2):
            pairs.append((ref.at[:, u * quarter : (u + 1) * quarter], raw_ref.at[n, u * NB : (u + 1) * NB]))
    bring(sem, pairs)
    norms = jnp.zeros((2 * NB, 1), jnp.float32)
    cross = jnp.zeros((2 * NB, NB), jnp.float32)
    for n, spot in enumerate(spots(where_ref, quarter)[:3]):
        weight = weight_ref[:, pl.ds(spot, quarter)]
        raw = raw_ref[n]
        wide = raw.astype(jnp.float32)
        scaled_ref[:, pl.ds(spot, quarter)] = (wide * weight).astype(jnp.bfloat16)
        norms += jnp.sum(wide * wide * weight, axis=1, keepdims=True)
        cross += dot_fast(raw, zero_ref[:, pl.ds(spot, quarter)], NT)
    norm_ref[...] = norms
    cross_ref[...] = cross


def far_kernel(where_ref, far0_ref, far1_ref, weight_ref, scaled0_ref, norm0_ref, x_ref, part_norm_ref, part_cross_ref,
               before_ref, scaled_ref, norm_ref, q_ref, raw_ref, zero_ref, out_ref, sem):
    quarter = far0_ref.shape[1] // 2
    spot = spots(where_ref, quarter)[3]
    pairs = [(scaled0_ref.at[:, pl.ds(spot, quarter)], zero_ref)]
    for u in range(2):
        part = slice(u * quarter, (u + 1) * quarter)
        pairs.append((far0_ref.at[:, part], raw_ref.at[u * NB : u * NB + NB // 2]))
        pairs.append((far1_ref.at[:, part], raw_ref.at[u * NB + NB // 2 : (u + 1) * NB]))
    bring(sem, pairs)
    weight = weight_ref[:, pl.ds(spot, quarter)]
    raw = raw_ref[...]
    wide = raw.astype(jnp.float32)
    out_ref[...] = (wide * weight).astype(jnp.bfloat16)
    back = pltpu.make_async_copy(out_ref, scaled_ref.at[:, pl.ds(spot, quarter)], sem.at[0])
    back.start()
    norms = part_norm_ref[...] + jnp.sum(wide * wide * weight, axis=1, keepdims=True)
    cross = part_cross_ref[...] + dot_fast(raw, zero_ref[...], NT)
    norm_ref[:, :NB] = norm0_ref[...]
    norm_ref[:, NB:] = as_row(norms)
    kern = jnp.exp(-0.5 * (norms + norm0_ref[...] - 2.0 * cross))
    store_triple(q_ref, dot_high(x_ref[...], kern, NT))
    back.wait()


def main_kernel(tiles, rows_dev, where_ref, rows_ref, norm_ref, w0_ref, wc_ref, wn_ref, nug_ref, inv_ref, q_ref, l_ref, o_ref):
    step = pl.program_id(0)
    row, col = where_ref[0], where_ref[1]
    eye = lax.broadcasted_iota(jnp.int32, (NB, NB), 0) == lax.broadcasted_iota(jnp.int32, (NB, NB), 1)
    for n in range(tiles):
        tile = (step * tiles + n) * rows_dev + row
        data = rows_ref[n * NB : (n + 1) * NB, :]
        cross = jnp.concatenate([dot_fast(data, w0_ref[...], NT), dot_fast(data, wc_ref[...], NT)], axis=1)
        norms = norm_ref[n * NB : (n + 1) * NB, :]
        kern = jnp.exp(-0.5 * (norms + wn_ref[...] - 2.0 * cross))
        left = kern[:, :NB] + jnp.where(eye & (tile == 0), nug_ref[:, :NB], 0.0)
        high, low = halves(left)
        panel = lax.dot_general(
            jnp.concatenate([high, high, low], axis=1), inv_ref[...], NN, preferred_element_type=jnp.float32
        )
        high, low = halves(panel)
        update = lax.dot_general(
            jnp.concatenate([high, high, low], axis=1), q_ref[...], NN, preferred_element_type=jnp.float32
        )
        first_tile = tile == 0
        for u in range(2):
            part = slice(NB * (u + 1), NB * (u + 2))
            own = kern[:, part] + jnp.where(eye & (tile == col + 32 * u), nug_ref[:, part], 0.0)
            result = jnp.where(first_tile, own, own - update[:, NB * u : NB * (u + 1)])
            if u == 0:
                result = jnp.where(col == 0, jnp.where(first_tile, l_ref[...], panel), result)
            for half in range(2):
                o_ref[pl.ds(n * NB * 4 + 2 * u + half, NB, stride=4), :] = result[:, 128 * half : 128 * (half + 1)]


def x_move(step):
    return [(y * 8 + x * 2 + k, y * 8 + (x + step) % 4 * 2 + k) for y in range(4) for x in range(4) for k in range(2)]


def y_move(step):
    return [(y * 8 + x * 2 + k, (y + step) % 4 * 8 + x * 2 + k) for y in range(4) for x in range(4) for k in range(2)]


def ring_join(value, moves):
    return jnp.concatenate([value] + [lax.ppermute(value, "col", moves(step)) for step in (1, -1, 2)], axis=0)


def local(samples, ard_weight, nugget):
    row_count = lax.axis_size("row")
    col_count = lax.axis_size("col")
    row_index = lax.axis_index("row")
    col_index = lax.axis_index("col")
    row_tiles, _, _, sub, features = samples.shape
    quarter = features // row_count
    fold = row_tiles // 2
    own = samples.reshape(row_tiles, sub, features)
    weight_row = ard_weight.reshape(1, features)
    f32, bf16 = jnp.float32, jnp.bfloat16
    shape = jax.ShapeDtypeStruct

    gathered = lax.all_gather(samples, "col", axis=2, tiled=True)

    widened = own.astype(f32)
    own_norms = jnp.sum(widened * widened * ard_weight, axis=2)
    n_high = lax.reduce_precision(own_norms, 8, 7)
    n_mid = lax.reduce_precision(own_norms - n_high, 8, 7)
    n_low = own_norms - n_high - n_mid
    bits = jnp.stack([n_high, n_mid, n_low]).astype(bf16).transpose(2, 0, 1).reshape(sub, 3 * row_tiles)

    cut = own.reshape(row_tiles, sub, row_count, quarter).transpose(2, 0, 1, 3)
    extra = jnp.broadcast_to(nugget.reshape(1, row_tiles, sub, 1), (row_count, row_tiles, sub, 128))
    share = features // row_tiles
    zero = own[0].reshape(sub, row_tiles, share).transpose(1, 0, 2)
    zero = jnp.broadcast_to(zero[None], (row_count, row_tiles, sub, share))
    sent = lax.all_to_all(jnp.concatenate([cut, extra, zero], axis=3), "row", 0, 0)
    zero = sent[0, :, :, quarter + 128 :].transpose(1, 0, 2).reshape(sub, features)
    sent = sent[..., : quarter + 128].reshape(row_count, 2, fold, sub, quarter + 128).transpose(2, 0, 1, 3, 4)
    sent = sent.reshape(col_count, 2, sub, quarter + 128)

    core = col_index % 2
    chip_x, chip_y = col_index // 2 % 4, col_index // 8
    sibling = [(i, i ^ 1) for i in range(col_count)]
    left, right = zero[:, : features // 2], zero[:, features // 2 :]
    kept = jnp.where(core == 0, left, right)
    came = lax.ppermute(jnp.where(core == 0, right, left), "col", sibling)
    block = jnp.where(core == 0, jnp.concatenate([kept, came]), jnp.concatenate([came, kept]))
    line = ring_join(block[None], x_move)
    below, above = lax.ppermute(line, "col", y_move(1)), lax.ppermute(line, "col", y_move(-1))
    mine = jnp.concatenate(
        [line, below, above, lax.ppermute(below[:2], "col", y_move(1)), lax.ppermute(above[2:], "col", y_move(-1))])
    theirs = lax.ppermute(mine, "col", sibling)
    body = sent[..., :quarter]
    tags = sent[..., quarter]
    tail = jnp.concatenate(
        [jnp.broadcast_to(tags[0, 0][None, :, None], (col_count, sub, 1)),
         tags[:, 0, :, None], tags[:, 1, :, None],
         jnp.zeros((col_count, sub, 61), bf16),
         jnp.broadcast_to(bits[None], (col_count, sub, 3 * row_tiles)),
         jnp.zeros((col_count, sub, 64 - 3 * row_tiles), bf16)], axis=2)
    got = lax.all_to_all(jnp.concatenate([body[:, 0], body[:, 1], tail], axis=2), "col", 0, 0)
    got = got.reshape(NB, -1)
    tags = got[:, 2 * quarter :].astype(f32)
    nug = tags[:, :3].T.reshape(1, 3 * NB)
    norm_bits = tags[:, 64 : 64 + 3 * row_tiles].reshape(NB, 3, row_tiles)
    norms = ((norm_bits[:, 0] + norm_bits[:, 1]) + norm_bits[:, 2]).T

    up = [(i, (i + 1) % row_count) for i in range(row_count)]
    down = [(i, (i - 1) % row_count) for i in range(row_count)]

    ring_of = jnp.array(RING, jnp.int32)
    chips = lax.rem(chip_y + ring_of, 4)[:, None] * 4 + lax.rem(chip_x + ring_of, 4)[None, :]
    where = jnp.concatenate([jnp.stack([row_index, col_index]), chips.reshape(-1)]).astype(jnp.int32)
    norms = norms.reshape(-1, 1)

    cols = got[:, : 2 * quarter]
    below, above = lax.ppermute(cols, "row", up), lax.ppermute(cols, "row", down)
    scaled0, norms0, corner, inverse, inverse3 = pl.pallas_call(
        corner_kernel,
        out_shape=(shape((NB, features), bf16), shape((1, NB), f32), shape((NB, NB), f32), shape((NB, NB), f32),
                   shape((3 * NB, NB), bf16)),
        in_specs=[SMEM] + [HBM] * 2 + [VMEM] * 2,
        out_specs=(VMEM,) * 5,
        scratch_shapes=[pltpu.VMEM((NB, features), bf16), pltpu.VMEM((NB, NB), f32), pltpu.SemaphoreType.DMA((32,))],
        cost_estimate=SMALL,
        compiler_params=pltpu.CompilerParams(vmem_limit_bytes=GRANT),
    )(where, mine, theirs, weight_row, nug[:, :NB])
    corner, below, above = lax.optimization_barrier((corner, below, above))
    cols_far = (lax.ppermute(below[: NB // 2], "row", up), lax.ppermute(above[NB // 2 :], "row", down))
    limit = pltpu.CompilerParams(vmem_limit_bytes=GRANT)
    near = shape((2 * NB, features), bf16)
    scaled, norms_c, cross_c = pl.pallas_call(
        column_kernel,
        out_shape=(near, shape((2 * NB, 1), f32), shape((2 * NB, NB), f32)),
        in_specs=[SMEM] + [HBM] * 3 + [VMEM, HBM],
        out_specs=(VMEM,) * 3,
        scratch_shapes=[pltpu.VMEM((3, 2 * NB, quarter), bf16), pltpu.VMEM((NB, features), bf16),
                        pltpu.SemaphoreType.DMA((7,))],
        cost_estimate=SMALL,
        compiler_params=limit,
    )(where, cols, below, above, weight_row, scaled0)
    scaled, wn, q_panel = pl.pallas_call(
        far_kernel,
        out_shape=(near, shape((1, 3 * NB), f32), shape((3 * NB, 2 * NB), bf16)),
        in_specs=[SMEM] + [HBM] * 2 + [VMEM, HBM] + [VMEM] * 4 + [HBM],
        out_specs=(HBM, VMEM, VMEM),
        scratch_shapes=[pltpu.VMEM((2 * NB, quarter), bf16), pltpu.VMEM((NB, quarter), bf16),
                        pltpu.VMEM((2 * NB, quarter), bf16), pltpu.SemaphoreType.DMA((5,))],
        input_output_aliases={9: 0},
        cost_estimate=SMALL,
        compiler_params=limit,
    )(where, *cols_far, weight_row, scaled0, norms0, inverse, norms_c, cross_c, scaled)

    fixed = (scaled0, scaled, wn, nug, inverse3, q_panel, corner)

    def whole(value):
        return pl.BlockSpec(value.shape, lambda i, _: (0, 0), pipeline_mode=pl.Buffered(1))

    rows_data = gathered.reshape(row_tiles * NB, features)
    tiles = 2
    out = pl.pallas_call(
        functools.partial(main_kernel, tiles, 4),
        out_shape=shape((row_tiles * NB * 4, 128), f32),
        grid_spec=pltpu.PrefetchScalarGridSpec(
            num_scalar_prefetch=1,
            grid=(row_tiles // tiles,),
            in_specs=[
                pl.BlockSpec((tiles * NB, features), lambda i, _: (i, 0)),
                pl.BlockSpec((tiles * NB, 1), lambda i, _: (i, 0)),
            ] + [whole(v) for v in fixed],
            out_specs=pl.BlockSpec((tiles * NB * 4, 128), lambda i, _: (i, 0)),
        ),
        compiler_params=pltpu.CompilerParams(vmem_limit_bytes=GRANT),
        cost_estimate=pl.CostEstimate(flops=30 * 10**9, bytes_accessed=48 * 2**20, transcendentals=0),
    )(where, rows_data, norms, *fixed)
    return out.reshape(row_tiles, 1, NB, 2, 1, NB)


def solution(mesh):
    placed = (P(None, "row", "col", None, None), P(), P(None, "row", "col", None))
    return jax.shard_map(
        local,
        mesh=mesh,
        in_specs=placed,
        out_specs=P(None, "row", None, None, "col", None),
        check_vma=False,
    )
```

```python
import functools

import jax
import jax.numpy as jnp
from jax import lax
from jax.experimental import pallas as pl
from jax.experimental.pallas import tpu as pltpu
from jax.sharding import PartitionSpec as P

NB = 256
HIGH = lax.Precision.HIGHEST
NT = (((1,), (1,)), ((), ()))
NN = (((1,), (0,)), ((), ()))
GRANT = 62 * 2**20
SMALL = pl.CostEstimate(flops=1, bytes_accessed=1, transcendentals=0)
VMEM = pl.BlockSpec(memory_space=pltpu.VMEM)
HBM = pl.BlockSpec(memory_space=pl.ANY)
SMEM = pl.BlockSpec(memory_space=pltpu.SMEM)


def dot_high(left, right, dims=NN):
    return lax.dot_general(left, right, dims, precision=HIGH, preferred_element_type=jnp.float32)


def dot_fast(left, right, dims):
    return lax.dot_general(left, right, dims, preferred_element_type=jnp.float32)


def halves(value):
    high = value.astype(jnp.bfloat16)
    low = (value - high.astype(jnp.float32)).astype(jnp.bfloat16)
    return high, low


def as_row(column):
    return jnp.broadcast_to(column, (column.shape[0], 128)).T[0:1, :]


def eliminate(block):
    size = block.shape[0]
    height = 32
    rows = lax.broadcasted_iota(jnp.int32, (size, size), 0)
    cols = lax.broadcasted_iota(jnp.int32, (size, size), 1)
    parts = [block[g * height : (g + 1) * height] for g in range(size // height)]
    inner = lax.broadcasted_iota(jnp.int32, (height, 1), 0)
    lane = lax.broadcasted_iota(jnp.int32, (1, size), 1)

    def spread(value):
        return jnp.broadcast_to(value, (value.shape[0], size))

    for j in range(0, size, 2):
        first, at = divmod(j, height)
        row0 = parts[first][at : at + 1, :]
        row1 = parts[first][at + 1 : at + 2, :]
        a, b = spread(row0[:, j : j + 1]), spread(row0[:, j + 1 : j + 2])
        c, d = spread(row1[:, j : j + 1]), spread(row1[:, j + 1 : j + 2])
        inverse = 1.0 / a
        scale, ratio = c * inverse, b * inverse
        row0 = row0 + (lane == j).astype(jnp.float32)
        row1 = row1 - scale * row0 + (lane == j + 1).astype(jnp.float32)
        row1 = row1 * (1.0 / (d - scale * b))
        row0 = row0 * inverse
        for g in range(first, size // height):
            left = spread(parts[g][:, j : j + 1])
            right = spread(parts[g][:, j + 1 : j + 2]) - left * ratio
            if g == first:
                left = jnp.where(inner > at, left, 0.0)
                right = jnp.where(inner > at + 1, right, 0.0)
            parts[g] = parts[g] - left * row0 - right * row1
    whole = jnp.concatenate(parts, axis=0)
    eye = (rows == cols).astype(jnp.float32)
    pivots = jnp.sum(whole * eye, axis=1, keepdims=True)
    root = lax.rsqrt(pivots)
    root = root * (1.5 - 0.5 * pivots * root * root)
    return jnp.where(rows > cols, whole, eye) * root


def store_factor(a_ref, l_ref, x_ref):
    half = NB // 2
    rows = lax.broadcasted_iota(jnp.int32, (half, half), 0)
    cols = lax.broadcasted_iota(jnp.int32, (half, half), 1)
    lower = rows >= cols
    zero = jnp.zeros((half, half), jnp.float32)
    a11, a21, a22 = a_ref[:half, :half], a_ref[half:, :half], a_ref[half:, half:]
    x11 = eliminate(a11)
    l21 = dot_high(a21, x11, NT)
    l_ref[:half, :half] = jnp.where(lower, dot_high(a11, x11, NT), 0.0)
    l_ref[:half, half:] = zero
    l_ref[half:, :half] = l21
    s22 = a22 - dot_high(l21, l21, NT)
    x22 = eliminate(s22)
    l_ref[half:, half:] = jnp.where(lower, dot_high(s22, x22, NT), 0.0)
    x_ref[:half, :half] = x11
    x_ref[:half, half:] = zero
    x_ref[half:, :half] = -dot_high(x22, dot_high(l21, x11))
    x_ref[half:, half:] = x22


def store_triple(out_ref, value):
    high, low = halves(value)
    size = value.shape[0]
    out_ref[:size, :] = high
    out_ref[size : 2 * size, :] = low
    out_ref[2 * size :, :] = high


def spots(where_ref, quarter):
    row = where_ref[0]
    return [pl.multiple_of(lax.rem(row + 4 - d, 4) * quarter, quarter) for d in (0, 1, 3, 2)]


def bring(sem, pairs):
    copies = [pltpu.make_async_copy(source, target, sem.at[n]) for n, (source, target) in enumerate(pairs)]
    for copy in copies:
        copy.start()
    for copy in copies:
        copy.wait()


def corner_kernel(where_ref, mine_ref, theirs_ref, weight_ref, nug_ref,
                  scaled_ref, norm_ref, l_ref, x_ref, x3_ref, raw_ref, a_ref, sem):
    eighth = mine_ref.shape[1]
    quarter = 2 * eighth
    core = lax.rem(where_ref[1], 2)
    pairs = []
    for n, spot in enumerate(spots(where_ref, quarter)):
        for ref, side in ((mine_ref, core), (theirs_ref, 1 - core)):
            at = pl.multiple_of(spot + side * eighth, eighth)
            pairs.append((ref.at[n * NB : (n + 1) * NB], raw_ref.at[:, pl.ds(at, eighth)]))
    bring(sem, pairs)
    norms = jnp.zeros((NB, 1), jnp.float32)
    cross = jnp.zeros((NB, NB), jnp.float32)
    for j in range(4):
        part = slice(j * quarter, (j + 1) * quarter)
        raw = raw_ref[:, part]
        wide = raw.astype(jnp.float32)
        product = wide * weight_ref[:, part]
        scaled = product.astype(jnp.bfloat16)
        scaled_ref[:, part] = scaled
        norms += jnp.sum(wide * wide * weight_ref[:, part], axis=1, keepdims=True)
        cross += dot_fast(raw, scaled, NT)
    row_norms = as_row(norms)
    norm_ref[...] = row_norms
    eye = lax.broadcasted_iota(jnp.int32, (NB, NB), 0) == lax.broadcasted_iota(jnp.int32, (NB, NB), 1)
    tile = jnp.exp(-0.5 * (norms + row_norms - 2.0 * cross)) + jnp.where(eye, nug_ref[...], 0.0)
    a_ref[...] = 0.5 * (tile + tile.T)
    store_factor(a_ref, l_ref, x_ref)
    store_triple(x3_ref, x_ref[...].T)


def column_kernel(where_ref, own0_ref, own1_ref, below0_ref, below1_ref, above0_ref, above1_ref, weight_ref,
                  scaled0_ref, scaled_ref, norm_ref, cross_ref, raw_ref, zero_ref, sem):
    quarter = own0_ref.shape[1] // 2
    pairs = [(scaled0_ref, zero_ref)]
    for n, group in enumerate(((own0_ref, own1_ref), (below0_ref, below1_ref), (above0_ref, above1_ref))):
        for u in range(2):
            for side, ref in enumerate(group):
                rows = slice(u * NB + side * NB // 2, u * NB + (side + 1) * NB // 2)
                pairs.append((ref.at[:, u * quarter : (u + 1) * quarter], raw_ref.at[n, rows]))
    bring(sem, pairs)
    norms = jnp.zeros((2 * NB, 1), jnp.float32)
    cross = jnp.zeros((2 * NB, NB), jnp.float32)
    for n, spot in enumerate(spots(where_ref, quarter)[:3]):
        weight = weight_ref[:, pl.ds(spot, quarter)]
        raw = raw_ref[n]
        wide = raw.astype(jnp.float32)
        scaled_ref[:, pl.ds(spot, quarter)] = (wide * weight).astype(jnp.bfloat16)
        norms += jnp.sum(wide * wide * weight, axis=1, keepdims=True)
        cross += dot_fast(raw, zero_ref[:, pl.ds(spot, quarter)], NT)
    norm_ref[...] = norms
    cross_ref[...] = cross


def far_kernel(where_ref, far0_ref, far1_ref, weight_ref, scaled0_ref, norm0_ref, x_ref, part_norm_ref, part_cross_ref,
               before_ref, scaled_ref, norm_ref, q_ref, raw_ref, zero_ref, out_ref, sem):
    quarter = far0_ref.shape[1] // 2
    spot = spots(where_ref, quarter)[3]
    pairs = [(scaled0_ref.at[:, pl.ds(spot, quarter)], zero_ref)]
    for u in range(2):
        part = slice(u * quarter, (u + 1) * quarter)
        pairs.append((far0_ref.at[:, part], raw_ref.at[u * NB : u * NB + NB // 2]))
        pairs.append((far1_ref.at[:, part], raw_ref.at[u * NB + NB // 2 : (u + 1) * NB]))
    bring(sem, pairs)
    weight = weight_ref[:, pl.ds(spot, quarter)]
    raw = raw_ref[...]
    wide = raw.astype(jnp.float32)
    out_ref[...] = (wide * weight).astype(jnp.bfloat16)
    back = pltpu.make_async_copy(out_ref, scaled_ref.at[:, pl.ds(spot, quarter)], sem.at[0])
    back.start()
    norms = part_norm_ref[...] + jnp.sum(wide * wide * weight, axis=1, keepdims=True)
    cross = part_cross_ref[...] + dot_fast(raw, zero_ref[...], NT)
    norm_ref[:, :NB] = norm0_ref[...]
    norm_ref[:, NB:] = as_row(norms)
    kern = jnp.exp(-0.5 * (norms + norm0_ref[...] - 2.0 * cross))
    store_triple(q_ref, dot_high(x_ref[...], kern, NT))
    back.wait()


def main_kernel(tiles, rows_dev, where_ref, rows_ref, norm_ref, w0_ref, wc_ref, wn_ref, nug_ref, inv_ref, q_ref, l_ref, o_ref):
    step = pl.program_id(0)
    row, col = where_ref[0], where_ref[1]
    eye = lax.broadcasted_iota(jnp.int32, (NB, NB), 0) == lax.broadcasted_iota(jnp.int32, (NB, NB), 1)
    for n in range(tiles):
        tile = (step * tiles + n) * rows_dev + row
        data = rows_ref[n * NB : (n + 1) * NB, :]
        cross = jnp.concatenate([dot_fast(data, w0_ref[...], NT), dot_fast(data, wc_ref[...], NT)], axis=1)
        norms = norm_ref[n * NB : (n + 1) * NB, :]
        kern = jnp.exp(-0.5 * (norms + wn_ref[...] - 2.0 * cross))
        left = kern[:, :NB] + jnp.where(eye & (tile == 0), nug_ref[:, :NB], 0.0)
        high, low = halves(left)
        panel = lax.dot_general(
            jnp.concatenate([high, high, low], axis=1), inv_ref[...], NN, preferred_element_type=jnp.float32
        )
        high, low = halves(panel)
        update = lax.dot_general(
            jnp.concatenate([high, high, low], axis=1), q_ref[...], NN, preferred_element_type=jnp.float32
        )
        first_tile = tile == 0
        for u in range(2):
            part = slice(NB * (u + 1), NB * (u + 2))
            own = kern[:, part] + jnp.where(eye & (tile == col + 32 * u), nug_ref[:, part], 0.0)
            result = jnp.where(first_tile, own, own - update[:, NB * u : NB * (u + 1)])
            if u == 0:
                result = jnp.where(col == 0, jnp.where(first_tile, l_ref[...], panel), result)
            for half in range(2):
                o_ref[pl.ds(n * NB * 4 + 2 * u + half, NB, stride=4), :] = result[:, 128 * half : 128 * (half + 1)]


def local(samples, ard_weight, nugget):
    row_count = lax.axis_size("row")
    col_count = lax.axis_size("col")
    row_index = lax.axis_index("row")
    col_index = lax.axis_index("col")
    row_tiles, _, _, sub, features = samples.shape
    quarter = features // row_count
    fold = row_tiles // 2
    own = samples.reshape(row_tiles, sub, features)
    weight_row = ard_weight.reshape(1, features)
    f32, bf16 = jnp.float32, jnp.bfloat16
    shape = jax.ShapeDtypeStruct

    gathered = lax.all_gather(samples, "col", axis=2, tiled=True)

    widened = own.astype(f32)
    own_norms = jnp.sum(widened * widened * ard_weight, axis=2)
    n_high = lax.reduce_precision(own_norms, 8, 7)
    n_mid = lax.reduce_precision(own_norms - n_high, 8, 7)
    n_low = own_norms - n_high - n_mid
    bits = jnp.stack([n_high, n_mid, n_low]).astype(bf16).transpose(2, 0, 1).reshape(sub, 3 * row_tiles)

    cut = own.reshape(row_tiles, sub, row_count, quarter).transpose(2, 0, 1, 3)
    extra = jnp.broadcast_to(nugget.reshape(1, row_tiles, sub, 1), (row_count, row_tiles, sub, 128))
    sent = lax.all_to_all(jnp.concatenate([cut, extra], axis=3), "row", 0, 0)
    sent = sent.reshape(row_count, 2, fold, sub, quarter + 128).transpose(2, 0, 1, 3, 4)
    sent = sent.reshape(col_count, 2, sub, quarter + 128)

    body = sent[..., :quarter]
    tags = sent[..., quarter]
    tail = jnp.concatenate(
        [jnp.broadcast_to(tags[0, 0][None, :, None], (col_count, sub, 1)),
         tags[:, 0, :, None], tags[:, 1, :, None],
         jnp.zeros((col_count, sub, 61), bf16),
         jnp.broadcast_to(bits[None], (col_count, sub, 3 * row_tiles)),
         jnp.zeros((col_count, sub, 64 - 3 * row_tiles), bf16)], axis=2)
    eighth = quarter // 2
    zero = jnp.stack([body[0, 0, :, :eighth], body[0, 0, :, eighth:]])
    zero = jnp.broadcast_to(zero[None], (col_count // 2, 2, sub, eighth)).reshape(col_count, sub, eighth)
    payload = jnp.concatenate([body[:, 0], body[:, 1], zero, tail], axis=2)
    got = lax.all_to_all(payload, "col", 0, 0)
    got = got.reshape(NB, -1)
    tags = got[:, 2 * quarter + eighth :].astype(f32)
    nug = tags[:, :3].T.reshape(1, 3 * NB)
    norm_bits = tags[:, 64 : 64 + 3 * row_tiles].reshape(NB, 3, row_tiles)
    norms = ((norm_bits[:, 0] + norm_bits[:, 1]) + norm_bits[:, 2]).T

    up = [(i, (i + 1) % row_count) for i in range(row_count)]
    down = [(i, (i - 1) % row_count) for i in range(row_count)]

    where = jnp.stack([row_index, col_index]).astype(jnp.int32)
    norms = norms.reshape(-1, 1)

    zero = [got[: NB // 2, 2 * quarter : 2 * quarter + eighth], got[NB // 2 :, 2 * quarter : 2 * quarter + eighth]]
    below = [lax.ppermute(value, "row", up) for value in zero]
    above = [lax.ppermute(value, "row", down) for value in zero]
    far = [lax.ppermute(below[0], "row", up), lax.ppermute(above[1], "row", down)]
    far, got = lax.optimization_barrier((far, got))
    mine = jnp.concatenate([*zero, *below, *above, *far])
    theirs = lax.ppermute(mine, "col", [(i, i ^ 1) for i in range(col_count)])

    cols = [got[: NB // 2, : 2 * quarter], got[NB // 2 :, : 2 * quarter]]
    below = [lax.ppermute(value, "row", up) for value in cols]
    above = [lax.ppermute(value, "row", down) for value in cols]
    scaled0, norms0, corner, inverse, inverse3 = pl.pallas_call(
        corner_kernel,
        out_shape=(shape((NB, features), bf16), shape((1, NB), f32), shape((NB, NB), f32), shape((NB, NB), f32),
                   shape((3 * NB, NB), bf16)),
        in_specs=[SMEM] + [HBM] * 2 + [VMEM] * 2,
        out_specs=(VMEM,) * 5,
        scratch_shapes=[pltpu.VMEM((NB, features), bf16), pltpu.VMEM((NB, NB), f32), pltpu.SemaphoreType.DMA((8,))],
        cost_estimate=SMALL,
        compiler_params=pltpu.CompilerParams(vmem_limit_bytes=GRANT),
    )(where, mine, theirs, weight_row, nug[:, :NB])
    corner, below, above = lax.optimization_barrier((corner, below, above))
    cols_far = (lax.ppermute(below[0], "row", up), lax.ppermute(above[1], "row", down))
    limit = pltpu.CompilerParams(vmem_limit_bytes=GRANT)
    near = shape((2 * NB, features), bf16)
    scaled, norms_c, cross_c = pl.pallas_call(
        column_kernel,
        out_shape=(near, shape((2 * NB, 1), f32), shape((2 * NB, NB), f32)),
        in_specs=[SMEM] + [HBM] * 6 + [VMEM, HBM],
        out_specs=(VMEM,) * 3,
        scratch_shapes=[pltpu.VMEM((3, 2 * NB, quarter), bf16), pltpu.VMEM((NB, features), bf16),
                        pltpu.SemaphoreType.DMA((13,))],
        cost_estimate=SMALL,
        compiler_params=limit,
    )(where, *cols, *below, *above, weight_row, scaled0)
    scaled, wn, q_panel = pl.pallas_call(
        far_kernel,
        out_shape=(near, shape((1, 3 * NB), f32), shape((3 * NB, 2 * NB), bf16)),
        in_specs=[SMEM] + [HBM] * 2 + [VMEM, HBM] + [VMEM] * 4 + [HBM],
        out_specs=(HBM, VMEM, VMEM),
        scratch_shapes=[pltpu.VMEM((2 * NB, quarter), bf16), pltpu.VMEM((NB, quarter), bf16),
                        pltpu.VMEM((2 * NB, quarter), bf16), pltpu.SemaphoreType.DMA((5,))],
        input_output_aliases={9: 0},
        cost_estimate=SMALL,
        compiler_params=limit,
    )(where, *cols_far, weight_row, scaled0, norms0, inverse, norms_c, cross_c, scaled)

    fixed = (scaled0, scaled, wn, nug, inverse3, q_panel, corner)

    def whole(value):
        return pl.BlockSpec(value.shape, lambda i, _: (0, 0), pipeline_mode=pl.Buffered(1))

    rows_data = gathered.reshape(row_tiles * NB, features)
    tiles = 2
    out = pl.pallas_call(
        functools.partial(main_kernel, tiles, 4),
        out_shape=shape((row_tiles * NB * 4, 128), f32),
        grid_spec=pltpu.PrefetchScalarGridSpec(
            num_scalar_prefetch=1,
            grid=(row_tiles // tiles,),
            in_specs=[
                pl.BlockSpec((tiles * NB, features), lambda i, _: (i, 0)),
                pl.BlockSpec((tiles * NB, 1), lambda i, _: (i, 0)),
            ] + [whole(v) for v in fixed],
            out_specs=pl.BlockSpec((tiles * NB * 4, 128), lambda i, _: (i, 0)),
        ),
        compiler_params=pltpu.CompilerParams(vmem_limit_bytes=GRANT),
        cost_estimate=pl.CostEstimate(flops=30 * 10**9, bytes_accessed=48 * 2**20, transcendentals=0),
    )(where, rows_data, norms, *fixed)
    return out.reshape(row_tiles, 1, NB, 2, 1, NB)


def solution(mesh):
    placed = (P(None, "row", "col", None, None), P(), P(None, "row", "col", None))
    return jax.shard_map(
        local,
        mesh=mesh,
        in_specs=placed,
        out_specs=P(None, "row", None, None, "col", None),
        check_vma=False,
    )
```

```python
import functools

import jax
import jax.numpy as jnp
from jax import lax
from jax.experimental import pallas as pl
from jax.experimental.pallas import tpu as pltpu
from jax.sharding import PartitionSpec as P

NB = 256
HIGH = lax.Precision.HIGHEST
NT = (((1,), (1,)), ((), ()))
NN = (((1,), (0,)), ((), ()))
GRANT = 62 * 2**20
SMALL = pl.CostEstimate(flops=1, bytes_accessed=1, transcendentals=0)
VMEM = pl.BlockSpec(memory_space=pltpu.VMEM)
HBM = pl.BlockSpec(memory_space=pl.ANY)
SMEM = pl.BlockSpec(memory_space=pltpu.SMEM)


def dot_high(left, right, dims=NN):
    return lax.dot_general(left, right, dims, precision=HIGH, preferred_element_type=jnp.float32)


def dot_fast(left, right, dims):
    return lax.dot_general(left, right, dims, preferred_element_type=jnp.float32)


def halves(value):
    high = value.astype(jnp.bfloat16)
    low = (value - high.astype(jnp.float32)).astype(jnp.bfloat16)
    return high, low


def as_row(column):
    return jnp.broadcast_to(column, (column.shape[0], 128)).T[0:1, :]


def eliminate(block):
    size = block.shape[0]
    height = 32
    rows = lax.broadcasted_iota(jnp.int32, (size, size), 0)
    cols = lax.broadcasted_iota(jnp.int32, (size, size), 1)
    parts = [block[g * height : (g + 1) * height] for g in range(size // height)]
    inner = lax.broadcasted_iota(jnp.int32, (height, 1), 0)
    lane = lax.broadcasted_iota(jnp.int32, (1, size), 1)

    def spread(value):
        return jnp.broadcast_to(value, (value.shape[0], size))

    for j in range(0, size, 2):
        first, at = divmod(j, height)
        row0 = parts[first][at : at + 1, :]
        row1 = parts[first][at + 1 : at + 2, :]
        a, b = spread(row0[:, j : j + 1]), spread(row0[:, j + 1 : j + 2])
        c, d = spread(row1[:, j : j + 1]), spread(row1[:, j + 1 : j + 2])
        inverse = 1.0 / a
        scale, ratio = c * inverse, b * inverse
        row0 = row0 + (lane == j).astype(jnp.float32)
        row1 = row1 - scale * row0 + (lane == j + 1).astype(jnp.float32)
        row1 = row1 * (1.0 / (d - scale * b))
        row0 = row0 * inverse
        for g in range(first, size // height):
            left = spread(parts[g][:, j : j + 1])
            right = spread(parts[g][:, j + 1 : j + 2]) - left * ratio
            if g == first:
                left = jnp.where(inner > at, left, 0.0)
                right = jnp.where(inner > at + 1, right, 0.0)
            parts[g] = parts[g] - left * row0 - right * row1
    whole = jnp.concatenate(parts, axis=0)
    eye = (rows == cols).astype(jnp.float32)
    pivots = jnp.sum(whole * eye, axis=1, keepdims=True)
    root = lax.rsqrt(pivots)
    root = root * (1.5 - 0.5 * pivots * root * root)
    return jnp.where(rows > cols, whole, eye) * root


def store_factor(a_ref, l_ref, x_ref):
    half = NB // 2
    rows = lax.broadcasted_iota(jnp.int32, (half, half), 0)
    cols = lax.broadcasted_iota(jnp.int32, (half, half), 1)
    lower = rows >= cols
    zero = jnp.zeros((half, half), jnp.float32)
    a11, a21, a22 = a_ref[:half, :half], a_ref[half:, :half], a_ref[half:, half:]
    x11 = eliminate(a11)
    l21 = dot_high(a21, x11, NT)
    l_ref[:half, :half] = jnp.where(lower, dot_high(a11, x11, NT), 0.0)
    l_ref[:half, half:] = zero
    l_ref[half:, :half] = l21
    s22 = a22 - dot_high(l21, l21, NT)
    x22 = eliminate(s22)
    l_ref[half:, half:] = jnp.where(lower, dot_high(s22, x22, NT), 0.0)
    x_ref[:half, :half] = x11
    x_ref[:half, half:] = zero
    x_ref[half:, :half] = -dot_high(x22, dot_high(l21, x11))
    x_ref[half:, half:] = x22


def store_triple(out_ref, value):
    high, low = halves(value)
    size = value.shape[0]
    out_ref[:size, :] = high
    out_ref[size : 2 * size, :] = low
    out_ref[2 * size :, :] = high


def spots(where_ref, quarter):
    row = where_ref[0]
    return [pl.multiple_of(lax.rem(row + 4 - d, 4) * quarter, quarter) for d in (0, 1, 3, 2)]


def bring(sem, pairs):
    copies = [pltpu.make_async_copy(source, target, sem.at[n]) for n, (source, target) in enumerate(pairs)]
    for copy in copies:
        copy.start()
    for copy in copies:
        copy.wait()


def corner_kernel(where_ref, mine_ref, theirs_ref, weight_ref, nug_ref,
                  scaled_ref, norm_ref, l_ref, x_ref, raw_ref, a_ref, sem):
    eighth = mine_ref.shape[1]
    quarter = 2 * eighth
    core = lax.rem(where_ref[1], 2)
    pairs = []
    for n, spot in enumerate(spots(where_ref, quarter)):
        for ref, side in ((mine_ref, core), (theirs_ref, 1 - core)):
            at = pl.multiple_of(spot + side * eighth, eighth)
            pairs.append((ref.at[n * NB : (n + 1) * NB], raw_ref.at[:, pl.ds(at, eighth)]))
    bring(sem, pairs)
    norms = jnp.zeros((NB, 1), jnp.float32)
    cross = jnp.zeros((NB, NB), jnp.float32)
    for j in range(4):
        part = slice(j * quarter, (j + 1) * quarter)
        raw = raw_ref[:, part]
        wide = raw.astype(jnp.float32)
        product = wide * weight_ref[:, part]
        scaled = product.astype(jnp.bfloat16)
        scaled_ref[:, part] = scaled
        norms += jnp.sum(wide * wide * weight_ref[:, part], axis=1, keepdims=True)
        cross += dot_fast(raw, scaled, NT)
    row_norms = as_row(norms)
    norm_ref[...] = row_norms
    eye = lax.broadcasted_iota(jnp.int32, (NB, NB), 0) == lax.broadcasted_iota(jnp.int32, (NB, NB), 1)
    tile = jnp.exp(-0.5 * (norms + row_norms - 2.0 * cross)) + jnp.where(eye, nug_ref[...], 0.0)
    a_ref[...] = 0.5 * (tile + tile.T)
    store_factor(a_ref, l_ref, x_ref)


def column_kernel(where_ref, own0_ref, own1_ref, below0_ref, below1_ref, above0_ref, above1_ref, weight_ref,
                  scaled0_ref, scaled_ref, norm_ref, cross_ref, raw_ref, zero_ref, sem):
    quarter = own0_ref.shape[1] // 2
    pairs = [(scaled0_ref, zero_ref)]
    for n, group in enumerate(((own0_ref, own1_ref), (below0_ref, below1_ref), (above0_ref, above1_ref))):
        for u in range(2):
            for side, ref in enumerate(group):
                rows = slice(u * NB + side * NB // 2, u * NB + (side + 1) * NB // 2)
                pairs.append((ref.at[:, u * quarter : (u + 1) * quarter], raw_ref.at[n, rows]))
    bring(sem, pairs)
    norms = jnp.zeros((2 * NB, 1), jnp.float32)
    cross = jnp.zeros((2 * NB, NB), jnp.float32)
    for n, spot in enumerate(spots(where_ref, quarter)[:3]):
        weight = weight_ref[:, pl.ds(spot, quarter)]
        raw = raw_ref[n]
        wide = raw.astype(jnp.float32)
        scaled_ref[:, pl.ds(spot, quarter)] = (wide * weight).astype(jnp.bfloat16)
        norms += jnp.sum(wide * wide * weight, axis=1, keepdims=True)
        cross += dot_fast(raw, zero_ref[:, pl.ds(spot, quarter)], NT)
    norm_ref[...] = norms
    cross_ref[...] = cross


def far_kernel(where_ref, far0_ref, far1_ref, weight_ref, scaled0_ref, norm0_ref, x_ref, part_norm_ref, part_cross_ref,
               before_ref, scaled_ref, norm_ref, q_ref, raw_ref, zero_ref, out_ref, sem):
    quarter = far0_ref.shape[1] // 2
    spot = spots(where_ref, quarter)[3]
    pairs = [(scaled0_ref.at[:, pl.ds(spot, quarter)], zero_ref)]
    for u in range(2):
        part = slice(u * quarter, (u + 1) * quarter)
        pairs.append((far0_ref.at[:, part], raw_ref.at[u * NB : u * NB + NB // 2]))
        pairs.append((far1_ref.at[:, part], raw_ref.at[u * NB + NB // 2 : (u + 1) * NB]))
    bring(sem, pairs)
    weight = weight_ref[:, pl.ds(spot, quarter)]
    raw = raw_ref[...]
    wide = raw.astype(jnp.float32)
    out_ref[...] = (wide * weight).astype(jnp.bfloat16)
    back = pltpu.make_async_copy(out_ref, scaled_ref.at[:, pl.ds(spot, quarter)], sem.at[0])
    back.start()
    norms = part_norm_ref[...] + jnp.sum(wide * wide * weight, axis=1, keepdims=True)
    cross = part_cross_ref[...] + dot_fast(raw, zero_ref[...], NT)
    norm_ref[:, :NB] = norm0_ref[...]
    norm_ref[:, NB:] = as_row(norms)
    kern = jnp.exp(-0.5 * (norms + norm0_ref[...] - 2.0 * cross))
    turned = x_ref[...].T
    solved = dot_high(turned, dot_high(x_ref[...], kern, NT))
    store_triple(q_ref, jnp.concatenate(
        [jnp.where(where_ref[1] == 0, turned, solved[:, :NB]), solved[:, NB:]], axis=1))
    back.wait()


def main_kernel(tiles, rows_dev, where_ref, rows_ref, norm_ref, w0_ref, wc_ref, wn_ref, nug_ref, q_ref, l_ref, o_ref):
    step = pl.program_id(0)
    row, col = where_ref[0], where_ref[1]
    eye = lax.broadcasted_iota(jnp.int32, (NB, NB), 0) == lax.broadcasted_iota(jnp.int32, (NB, NB), 1)
    for n in range(tiles):
        tile = (step * tiles + n) * rows_dev + row
        data = rows_ref[n * NB : (n + 1) * NB, :]
        cross = jnp.concatenate([dot_fast(data, w0_ref[...], NT), dot_fast(data, wc_ref[...], NT)], axis=1)
        norms = norm_ref[n * NB : (n + 1) * NB, :]
        kern = jnp.exp(-0.5 * (norms + wn_ref[...] - 2.0 * cross))
        left = kern[:, :NB] + jnp.where(eye & (tile == 0), nug_ref[:, :NB], 0.0)
        high, low = halves(left)
        update = dot_fast(jnp.concatenate([high, high, low], axis=1), q_ref[...], NN)
        first_tile = tile == 0
        for u in range(2):
            part = slice(NB * (u + 1), NB * (u + 2))
            own = kern[:, part] + jnp.where(eye & (tile == col + 32 * u), nug_ref[:, part], 0.0)
            result = jnp.where(first_tile, own, own - update[:, NB * u : NB * (u + 1)])
            if u == 0:
                result = jnp.where(col == 0, jnp.where(first_tile, l_ref[...], update[:, :NB]), result)
            for half in range(2):
                o_ref[pl.ds(n * NB * 4 + 2 * u + half, NB, stride=4), :] = result[:, 128 * half : 128 * (half + 1)]


def local(samples, ard_weight, nugget):
    row_count = lax.axis_size("row")
    col_count = lax.axis_size("col")
    row_index = lax.axis_index("row")
    col_index = lax.axis_index("col")
    row_tiles, _, _, sub, features = samples.shape
    quarter = features // row_count
    fold = row_tiles // 2
    own = samples.reshape(row_tiles, sub, features)
    weight_row = ard_weight.reshape(1, features)
    f32, bf16 = jnp.float32, jnp.bfloat16
    shape = jax.ShapeDtypeStruct

    gathered = lax.all_gather(samples, "col", axis=2, tiled=True)

    widened = own.astype(f32)
    own_norms = jnp.sum(widened * widened * ard_weight, axis=2)
    n_high = lax.reduce_precision(own_norms, 8, 7)
    n_mid = lax.reduce_precision(own_norms - n_high, 8, 7)
    n_low = own_norms - n_high - n_mid
    bits = jnp.stack([n_high, n_mid, n_low]).astype(bf16).transpose(2, 0, 1).reshape(sub, 3 * row_tiles)

    cut = own.reshape(row_tiles, sub, row_count, quarter).transpose(2, 0, 1, 3)
    extra = jnp.broadcast_to(nugget.reshape(1, row_tiles, sub, 1), (row_count, row_tiles, sub, 128))
    sent = lax.all_to_all(jnp.concatenate([cut, extra], axis=3), "row", 0, 0)
    sent = sent.reshape(row_count, 2, fold, sub, quarter + 128).transpose(2, 0, 1, 3, 4)
    sent = sent.reshape(col_count, 2, sub, quarter + 128)

    body = sent[..., :quarter]
    tags = sent[..., quarter]
    tail = jnp.concatenate(
        [jnp.broadcast_to(tags[0, 0][None, :, None], (col_count, sub, 1)),
         tags[:, 0, :, None], tags[:, 1, :, None],
         jnp.zeros((col_count, sub, 61), bf16),
         jnp.broadcast_to(bits[None], (col_count, sub, 3 * row_tiles)),
         jnp.zeros((col_count, sub, 64 - 3 * row_tiles), bf16)], axis=2)
    eighth = quarter // 2
    zero = jnp.stack([body[0, 0, :, :eighth], body[0, 0, :, eighth:]])
    zero = jnp.broadcast_to(zero[None], (col_count // 2, 2, sub, eighth)).reshape(col_count, sub, eighth)
    payload = jnp.concatenate([body[:, 0], body[:, 1], zero, tail], axis=2)
    got = lax.all_to_all(payload, "col", 0, 0)
    got = got.reshape(NB, -1)
    tags = got[:, 2 * quarter + eighth :].astype(f32)
    nug = tags[:, :3].T.reshape(1, 3 * NB)
    norm_bits = tags[:, 64 : 64 + 3 * row_tiles].reshape(NB, 3, row_tiles)
    norms = ((norm_bits[:, 0] + norm_bits[:, 1]) + norm_bits[:, 2]).T

    up = [(i, (i + 1) % row_count) for i in range(row_count)]
    down = [(i, (i - 1) % row_count) for i in range(row_count)]

    where = jnp.stack([row_index, col_index]).astype(jnp.int32)
    norms = norms.reshape(-1, 1)

    zero = [got[: NB // 2, 2 * quarter : 2 * quarter + eighth], got[NB // 2 :, 2 * quarter : 2 * quarter + eighth]]
    below = [lax.ppermute(value, "row", up) for value in zero]
    above = [lax.ppermute(value, "row", down) for value in zero]
    far = [lax.ppermute(below[0], "row", up), lax.ppermute(above[1], "row", down)]
    far, got = lax.optimization_barrier((far, got))
    mine = jnp.concatenate([*zero, *below, *above, *far])
    theirs = lax.ppermute(mine, "col", [(i, i ^ 1) for i in range(col_count)])

    cols = [got[: NB // 2, : 2 * quarter], got[NB // 2 :, : 2 * quarter]]
    below = [lax.ppermute(value, "row", up) for value in cols]
    above = [lax.ppermute(value, "row", down) for value in cols]
    scaled0, norms0, corner, inverse = pl.pallas_call(
        corner_kernel,
        out_shape=(shape((NB, features), bf16), shape((1, NB), f32), shape((NB, NB), f32), shape((NB, NB), f32)),
        in_specs=[SMEM] + [HBM] * 2 + [VMEM] * 2,
        out_specs=(VMEM,) * 4,
        scratch_shapes=[pltpu.VMEM((NB, features), bf16), pltpu.VMEM((NB, NB), f32), pltpu.SemaphoreType.DMA((8,))],
        cost_estimate=SMALL,
        compiler_params=pltpu.CompilerParams(vmem_limit_bytes=GRANT),
    )(where, mine, theirs, weight_row, nug[:, :NB])
    corner, below, above = lax.optimization_barrier((corner, below, above))
    cols_far = (lax.ppermute(below[0], "row", up), lax.ppermute(above[1], "row", down))
    limit = pltpu.CompilerParams(vmem_limit_bytes=GRANT)
    near = shape((2 * NB, features), bf16)
    scaled, norms_c, cross_c = pl.pallas_call(
        column_kernel,
        out_shape=(near, shape((2 * NB, 1), f32), shape((2 * NB, NB), f32)),
        in_specs=[SMEM] + [HBM] * 6 + [VMEM, HBM],
        out_specs=(VMEM,) * 3,
        scratch_shapes=[pltpu.VMEM((3, 2 * NB, quarter), bf16), pltpu.VMEM((NB, features), bf16),
                        pltpu.SemaphoreType.DMA((13,))],
        cost_estimate=SMALL,
        compiler_params=limit,
    )(where, *cols, *below, *above, weight_row, scaled0)
    scaled, wn, q_panel = pl.pallas_call(
        far_kernel,
        out_shape=(near, shape((1, 3 * NB), f32), shape((3 * NB, 2 * NB), bf16)),
        in_specs=[SMEM] + [HBM] * 2 + [VMEM, HBM] + [VMEM] * 4 + [HBM],
        out_specs=(HBM, VMEM, VMEM),
        scratch_shapes=[pltpu.VMEM((2 * NB, quarter), bf16), pltpu.VMEM((NB, quarter), bf16),
                        pltpu.VMEM((2 * NB, quarter), bf16), pltpu.SemaphoreType.DMA((5,))],
        input_output_aliases={9: 0},
        cost_estimate=SMALL,
        compiler_params=limit,
    )(where, *cols_far, weight_row, scaled0, norms0, inverse, norms_c, cross_c, scaled)

    fixed = (scaled0, scaled, wn, nug, q_panel, corner)

    def whole(value):
        return pl.BlockSpec(value.shape, lambda i, _: (0, 0), pipeline_mode=pl.Buffered(1))

    rows_data = gathered.reshape(row_tiles * NB, features)
    tiles = 2
    out = pl.pallas_call(
        functools.partial(main_kernel, tiles, 4),
        out_shape=shape((row_tiles * NB * 4, 128), f32),
        grid_spec=pltpu.PrefetchScalarGridSpec(
            num_scalar_prefetch=1,
            grid=(row_tiles // tiles,),
            in_specs=[
                pl.BlockSpec((tiles * NB, features), lambda i, _: (i, 0)),
                pl.BlockSpec((tiles * NB, 1), lambda i, _: (i, 0)),
            ] + [whole(v) for v in fixed],
            out_specs=pl.BlockSpec((tiles * NB * 4, 128), lambda i, _: (i, 0)),
        ),
        compiler_params=pltpu.CompilerParams(vmem_limit_bytes=GRANT),
        cost_estimate=pl.CostEstimate(flops=30 * 10**9, bytes_accessed=48 * 2**20, transcendentals=0),
    )(where, rows_data, norms, *fixed)
    return out.reshape(row_tiles, 1, NB, 2, 1, NB)


def solution(mesh):
    placed = (P(None, "row", "col", None, None), P(), P(None, "row", "col", None))
    return jax.shard_map(
        local,
        mesh=mesh,
        in_specs=placed,
        out_specs=P(None, "row", None, None, "col", None),
        check_vma=False,
    )
```

```python
import functools

import jax
import jax.numpy as jnp
from jax import lax
from jax.experimental import pallas as pl
from jax.experimental.pallas import tpu as pltpu
from jax.sharding import PartitionSpec as P

NB = 256
HIGH = lax.Precision.HIGHEST
NT = (((1,), (1,)), ((), ()))
NN = (((1,), (0,)), ((), ()))
GRANT = 62 * 2**20
SMALL = pl.CostEstimate(flops=1, bytes_accessed=1, transcendentals=0)
VMEM = pl.BlockSpec(memory_space=pltpu.VMEM)
HBM = pl.BlockSpec(memory_space=pl.ANY)
SMEM = pl.BlockSpec(memory_space=pltpu.SMEM)


def dot_high(left, right, dims=NN):
    return lax.dot_general(left, right, dims, precision=HIGH, preferred_element_type=jnp.float32)


def dot_fast(left, right, dims):
    return lax.dot_general(left, right, dims, preferred_element_type=jnp.float32)


def halves(value):
    high = value.astype(jnp.bfloat16)
    low = (value - high.astype(jnp.float32)).astype(jnp.bfloat16)
    return high, low


def as_row(column):
    return jnp.broadcast_to(column, (column.shape[0], 128)).T[0:1, :]


def eliminate(block):
    size = block.shape[0]
    height = 32
    rows = lax.broadcasted_iota(jnp.int32, (size, size), 0)
    cols = lax.broadcasted_iota(jnp.int32, (size, size), 1)
    parts = [block[g * height : (g + 1) * height] for g in range(size // height)]
    inner = lax.broadcasted_iota(jnp.int32, (height, 1), 0)
    lane = lax.broadcasted_iota(jnp.int32, (1, size), 1)

    def spread(value):
        return jnp.broadcast_to(value, (value.shape[0], size))

    for j in range(0, size, 2):
        first, at = divmod(j, height)
        row0 = parts[first][at : at + 1, :]
        row1 = parts[first][at + 1 : at + 2, :]
        a, b = spread(row0[:, j : j + 1]), spread(row0[:, j + 1 : j + 2])
        c, d = spread(row1[:, j : j + 1]), spread(row1[:, j + 1 : j + 2])
        inverse = 1.0 / a
        scale, ratio = c * inverse, b * inverse
        row0 = row0 + (lane == j).astype(jnp.float32)
        row1 = row1 - scale * row0 + (lane == j + 1).astype(jnp.float32)
        row1 = row1 * (1.0 / (d - scale * b))
        row0 = row0 * inverse
        for g in range(first, size // height):
            left = spread(parts[g][:, j : j + 1])
            right = spread(parts[g][:, j + 1 : j + 2]) - left * ratio
            if g == first:
                left = jnp.where(inner > at, left, 0.0)
                right = jnp.where(inner > at + 1, right, 0.0)
            parts[g] = parts[g] - left * row0 - right * row1
    whole = jnp.concatenate(parts, axis=0)
    eye = (rows == cols).astype(jnp.float32)
    pivots = jnp.sum(whole * eye, axis=1, keepdims=True)
    root = lax.rsqrt(pivots)
    root = root * (1.5 - 0.5 * pivots * root * root)
    return jnp.where(rows > cols, whole, eye) * root


def store_factor(a_ref, l_ref, x_ref):
    half = NB // 2
    rows = lax.broadcasted_iota(jnp.int32, (half, half), 0)
    cols = lax.broadcasted_iota(jnp.int32, (half, half), 1)
    lower = rows >= cols
    zero = jnp.zeros((half, half), jnp.float32)
    a11, a21, a22 = a_ref[:half, :half], a_ref[half:, :half], a_ref[half:, half:]
    x11 = eliminate(a11)
    l21 = dot_high(a21, x11, NT)
    l_ref[:half, :half] = jnp.where(lower, dot_high(a11, x11, NT), 0.0)
    l_ref[:half, half:] = zero
    l_ref[half:, :half] = l21
    s22 = a22 - dot_high(l21, l21, NT)
    x22 = eliminate(s22)
    l_ref[half:, half:] = jnp.where(lower, dot_high(s22, x22, NT), 0.0)
    x_ref[:half, :half] = x11
    x_ref[:half, half:] = zero
    x_ref[half:, :half] = -dot_high(x22, dot_high(l21, x11))
    x_ref[half:, half:] = x22


def store_triple(out_ref, value):
    high, low = halves(value)
    size = value.shape[0]
    out_ref[:size, :] = high
    out_ref[size : 2 * size, :] = low
    out_ref[2 * size :, :] = high


def spots(where_ref, quarter):
    row = where_ref[0]
    return [pl.multiple_of(lax.rem(row + 4 - d, 4) * quarter, quarter) for d in (0, 1, 3, 2)]


def bring(sem, pairs):
    copies = [pltpu.make_async_copy(source, target, sem.at[n]) for n, (source, target) in enumerate(pairs)]
    for copy in copies:
        copy.start()
    for copy in copies:
        copy.wait()


def corner_kernel(where_ref, mine_ref, theirs_ref, weight_ref, nug_ref,
                  scaled_ref, norm_ref, l_ref, x_ref, turned_ref, raw_ref, a_ref, sem):
    eighth = mine_ref.shape[1]
    quarter = 2 * eighth
    core = lax.rem(where_ref[1], 2)
    pairs = []
    for n, spot in enumerate(spots(where_ref, quarter)):
        for ref, side in ((mine_ref, core), (theirs_ref, 1 - core)):
            at = pl.multiple_of(spot + side * eighth, eighth)
            pairs.append((ref.at[n * NB : (n + 1) * NB], raw_ref.at[:, pl.ds(at, eighth)]))
    bring(sem, pairs)
    norms = jnp.zeros((NB, 1), jnp.float32)
    cross = jnp.zeros((NB, NB), jnp.float32)
    for j in range(4):
        part = slice(j * quarter, (j + 1) * quarter)
        raw = raw_ref[:, part]
        wide = raw.astype(jnp.float32)
        product = wide * weight_ref[:, part]
        scaled = product.astype(jnp.bfloat16)
        scaled_ref[:, part] = scaled
        norms += jnp.sum(wide * wide * weight_ref[:, part], axis=1, keepdims=True)
        cross += dot_fast(raw, scaled, NT)
    row_norms = as_row(norms)
    norm_ref[...] = row_norms
    eye = lax.broadcasted_iota(jnp.int32, (NB, NB), 0) == lax.broadcasted_iota(jnp.int32, (NB, NB), 1)
    tile = jnp.exp(-0.5 * (norms + row_norms - 2.0 * cross)) + jnp.where(eye, nug_ref[...], 0.0)
    a_ref[...] = 0.5 * (tile + tile.T)
    store_factor(a_ref, l_ref, x_ref)
    turned_ref[...] = x_ref[...].T


def column_kernel(where_ref, own0_ref, own1_ref, below0_ref, below1_ref, above0_ref, above1_ref, weight_ref,
                  scaled0_ref, scaled_ref, norm_ref, cross_ref, raw_ref, zero_ref, sem):
    quarter = own0_ref.shape[1] // 2
    pairs = [(scaled0_ref, zero_ref)]
    for n, group in enumerate(((own0_ref, own1_ref), (below0_ref, below1_ref), (above0_ref, above1_ref))):
        for u in range(2):
            for side, ref in enumerate(group):
                rows = slice(u * NB + side * NB // 2, u * NB + (side + 1) * NB // 2)
                pairs.append((ref.at[:, u * quarter : (u + 1) * quarter], raw_ref.at[n, rows]))
    bring(sem, pairs)
    norms = jnp.zeros((2 * NB, 1), jnp.float32)
    cross = jnp.zeros((2 * NB, NB), jnp.float32)
    for n, spot in enumerate(spots(where_ref, quarter)[:3]):
        weight = weight_ref[:, pl.ds(spot, quarter)]
        raw = raw_ref[n]
        wide = raw.astype(jnp.float32)
        scaled_ref[:, pl.ds(spot, quarter)] = (wide * weight).astype(jnp.bfloat16)
        norms += jnp.sum(wide * wide * weight, axis=1, keepdims=True)
        cross += dot_fast(raw, zero_ref[:, pl.ds(spot, quarter)], NT)
    norm_ref[...] = norms
    cross_ref[...] = cross


def far_kernel(where_ref, far0_ref, far1_ref, weight_ref, scaled0_ref, norm0_ref, x_ref, turned_ref, part_norm_ref, part_cross_ref,
               before_ref, scaled_ref, norm_ref, q_ref, raw_ref, zero_ref, out_ref, sem):
    quarter = far0_ref.shape[1] // 2
    spot = spots(where_ref, quarter)[3]
    pairs = [(scaled0_ref.at[:, pl.ds(spot, quarter)], zero_ref)]
    for u in range(2):
        part = slice(u * quarter, (u + 1) * quarter)
        pairs.append((far0_ref.at[:, part], raw_ref.at[u * NB : u * NB + NB // 2]))
        pairs.append((far1_ref.at[:, part], raw_ref.at[u * NB + NB // 2 : (u + 1) * NB]))
    bring(sem, pairs)
    weight = weight_ref[:, pl.ds(spot, quarter)]
    raw = raw_ref[...]
    wide = raw.astype(jnp.float32)
    out_ref[...] = (wide * weight).astype(jnp.bfloat16)
    back = pltpu.make_async_copy(out_ref, scaled_ref.at[:, pl.ds(spot, quarter)], sem.at[0])
    back.start()
    norms = part_norm_ref[...] + jnp.sum(wide * wide * weight, axis=1, keepdims=True)
    cross = part_cross_ref[...] + dot_fast(raw, zero_ref[...], NT)
    norm_ref[:, :NB] = norm0_ref[...]
    norm_ref[:, NB:] = as_row(norms)
    kern = jnp.exp(-0.5 * (norms + norm0_ref[...] - 2.0 * cross))
    turned = turned_ref[...]
    solved = dot_high(turned, dot_high(x_ref[...], kern, NT))
    store_triple(q_ref, jnp.concatenate(
        [jnp.where(where_ref[1] == 0, turned, solved[:, :NB]), solved[:, NB:]], axis=1))
    back.wait()


def main_kernel(tiles, rows_dev, where_ref, rows_ref, norm_ref, w0_ref, wc_ref, wn_ref, nug_ref, q_ref, l_ref, o_ref):
    step = pl.program_id(0)
    row, col = where_ref[0], where_ref[1]
    eye = lax.broadcasted_iota(jnp.int32, (NB, NB), 0) == lax.broadcasted_iota(jnp.int32, (NB, NB), 1)
    for n in range(tiles):
        tile = (step * tiles + n) * rows_dev + row
        data = rows_ref[n * NB : (n + 1) * NB, :]
        cross = jnp.concatenate([dot_fast(data, w0_ref[...], NT), dot_fast(data, wc_ref[...], NT)], axis=1)
        norms = norm_ref[n * NB : (n + 1) * NB, :]
        kern = jnp.exp(-0.5 * (norms + wn_ref[...] - 2.0 * cross))
        left = kern[:, :NB] + jnp.where(eye & (tile == 0), nug_ref[:, :NB], 0.0)
        high, low = halves(left)
        update = dot_fast(jnp.concatenate([high, high, low], axis=1), q_ref[...], NN)
        first_tile = tile == 0
        for u in range(2):
            part = slice(NB * (u + 1), NB * (u + 2))
            own = kern[:, part] + jnp.where(eye & (tile == col + 32 * u), nug_ref[:, part], 0.0)
            result = jnp.where(first_tile, own, own - update[:, NB * u : NB * (u + 1)])
            if u == 0:
                result = jnp.where(col == 0, jnp.where(first_tile, l_ref[...], update[:, :NB]), result)
            for half in range(2):
                o_ref[pl.ds(n * NB * 4 + 2 * u + half, NB, stride=4), :] = result[:, 128 * half : 128 * (half + 1)]


def local(samples, ard_weight, nugget):
    row_count = lax.axis_size("row")
    col_count = lax.axis_size("col")
    row_index = lax.axis_index("row")
    col_index = lax.axis_index("col")
    row_tiles, _, _, sub, features = samples.shape
    quarter = features // row_count
    fold = row_tiles // 2
    own = samples.reshape(row_tiles, sub, features)
    weight_row = ard_weight.reshape(1, features)
    f32, bf16 = jnp.float32, jnp.bfloat16
    shape = jax.ShapeDtypeStruct

    gathered = lax.all_gather(samples, "col", axis=2, tiled=True)

    widened = own.astype(f32)
    own_norms = jnp.sum(widened * widened * ard_weight, axis=2)
    n_high = lax.reduce_precision(own_norms, 8, 7)
    n_mid = lax.reduce_precision(own_norms - n_high, 8, 7)
    n_low = own_norms - n_high - n_mid
    bits = jnp.stack([n_high, n_mid, n_low]).astype(bf16).transpose(2, 0, 1).reshape(sub, 3 * row_tiles)

    cut = own.reshape(row_tiles, sub, row_count, quarter).transpose(2, 0, 1, 3)
    extra = jnp.broadcast_to(nugget.reshape(1, row_tiles, sub, 1), (row_count, row_tiles, sub, 128))
    sent = lax.all_to_all(jnp.concatenate([cut, extra], axis=3), "row", 0, 0)
    sent = sent.reshape(row_count, 2, fold, sub, quarter + 128).transpose(2, 0, 1, 3, 4)
    sent = sent.reshape(col_count, 2, sub, quarter + 128)

    body = sent[..., :quarter]
    tags = sent[..., quarter]
    tail = jnp.concatenate(
        [jnp.broadcast_to(tags[0, 0][None, :, None], (col_count, sub, 1)),
         tags[:, 0, :, None], tags[:, 1, :, None],
         jnp.zeros((col_count, sub, 61), bf16),
         jnp.broadcast_to(bits[None], (col_count, sub, 3 * row_tiles)),
         jnp.zeros((col_count, sub, 64 - 3 * row_tiles), bf16)], axis=2)
    eighth = quarter // 2
    zero = jnp.stack([body[0, 0, :, :eighth], body[0, 0, :, eighth:]])
    zero = jnp.broadcast_to(zero[None], (col_count // 2, 2, sub, eighth)).reshape(col_count, sub, eighth)
    payload = jnp.concatenate([body[:, 0], body[:, 1], zero, tail], axis=2)
    got = lax.all_to_all(payload, "col", 0, 0)
    got = got.reshape(NB, -1)
    tags = got[:, 2 * quarter + eighth :].astype(f32)
    nug = tags[:, :3].T.reshape(1, 3 * NB)
    norm_bits = tags[:, 64 : 64 + 3 * row_tiles].reshape(NB, 3, row_tiles)
    norms = ((norm_bits[:, 0] + norm_bits[:, 1]) + norm_bits[:, 2]).T

    up = [(i, (i + 1) % row_count) for i in range(row_count)]
    down = [(i, (i - 1) % row_count) for i in range(row_count)]

    where = jnp.stack([row_index, col_index]).astype(jnp.int32)
    norms = norms.reshape(-1, 1)

    zero = [got[: NB // 2, 2 * quarter : 2 * quarter + eighth], got[NB // 2 :, 2 * quarter : 2 * quarter + eighth]]
    below = [lax.ppermute(value, "row", up) for value in zero]
    above = [lax.ppermute(value, "row", down) for value in zero]
    far = [lax.ppermute(below[0], "row", up), lax.ppermute(above[1], "row", down)]
    far, got = lax.optimization_barrier((far, got))
    mine = jnp.concatenate([*zero, *below, *above, *far])
    theirs = lax.ppermute(mine, "col", [(i, i ^ 1) for i in range(col_count)])

    cols = [got[: NB // 2, : 2 * quarter], got[NB // 2 :, : 2 * quarter]]
    below = [lax.ppermute(value, "row", up) for value in cols]
    above = [lax.ppermute(value, "row", down) for value in cols]
    scaled0, norms0, corner, inverse, turned = pl.pallas_call(
        corner_kernel,
        out_shape=(shape((NB, features), bf16), shape((1, NB), f32), shape((NB, NB), f32), shape((NB, NB), f32),
                   shape((NB, NB), f32)),
        in_specs=[SMEM] + [HBM] * 2 + [VMEM] * 2,
        out_specs=(VMEM,) * 5,
        scratch_shapes=[pltpu.VMEM((NB, features), bf16), pltpu.VMEM((NB, NB), f32), pltpu.SemaphoreType.DMA((8,))],
        cost_estimate=SMALL,
        compiler_params=pltpu.CompilerParams(vmem_limit_bytes=GRANT),
    )(where, mine, theirs, weight_row, nug[:, :NB])
    corner, below, above = lax.optimization_barrier((corner, below, above))
    cols_far = (lax.ppermute(below[0], "row", up), lax.ppermute(above[1], "row", down))
    limit = pltpu.CompilerParams(vmem_limit_bytes=GRANT)
    near = shape((2 * NB, features), bf16)
    scaled, norms_c, cross_c = pl.pallas_call(
        column_kernel,
        out_shape=(near, shape((2 * NB, 1), f32), shape((2 * NB, NB), f32)),
        in_specs=[SMEM] + [HBM] * 6 + [VMEM, HBM],
        out_specs=(VMEM,) * 3,
        scratch_shapes=[pltpu.VMEM((3, 2 * NB, quarter), bf16), pltpu.VMEM((NB, features), bf16),
                        pltpu.SemaphoreType.DMA((13,))],
        cost_estimate=SMALL,
        compiler_params=limit,
    )(where, *cols, *below, *above, weight_row, scaled0)
    scaled, wn, q_panel = pl.pallas_call(
        far_kernel,
        out_shape=(near, shape((1, 3 * NB), f32), shape((3 * NB, 2 * NB), bf16)),
        in_specs=[SMEM] + [HBM] * 2 + [VMEM, HBM] + [VMEM] * 5 + [HBM],
        out_specs=(HBM, VMEM, VMEM),
        scratch_shapes=[pltpu.VMEM((2 * NB, quarter), bf16), pltpu.VMEM((NB, quarter), bf16),
                        pltpu.VMEM((2 * NB, quarter), bf16), pltpu.SemaphoreType.DMA((5,))],
        input_output_aliases={10: 0},
        cost_estimate=SMALL,
        compiler_params=limit,
    )(where, *cols_far, weight_row, scaled0, norms0, inverse, turned, norms_c, cross_c, scaled)

    fixed = (scaled0, scaled, wn, nug, q_panel, corner)

    def whole(value):
        return pl.BlockSpec(value.shape, lambda i, _: (0, 0), pipeline_mode=pl.Buffered(1))

    rows_data = gathered.reshape(row_tiles * NB, features)
    tiles = 2
    out = pl.pallas_call(
        functools.partial(main_kernel, tiles, 4),
        out_shape=shape((row_tiles * NB * 4, 128), f32),
        grid_spec=pltpu.PrefetchScalarGridSpec(
            num_scalar_prefetch=1,
            grid=(row_tiles // tiles,),
            in_specs=[
                pl.BlockSpec((tiles * NB, features), lambda i, _: (i, 0)),
                pl.BlockSpec((tiles * NB, 1), lambda i, _: (i, 0)),
            ] + [whole(v) for v in fixed],
            out_specs=pl.BlockSpec((tiles * NB * 4, 128), lambda i, _: (i, 0)),
        ),
        compiler_params=pltpu.CompilerParams(vmem_limit_bytes=GRANT),
        cost_estimate=pl.CostEstimate(flops=30 * 10**9, bytes_accessed=48 * 2**20, transcendentals=0),
    )(where, rows_data, norms, *fixed)
    return out.reshape(row_tiles, 1, NB, 2, 1, NB)


def solution(mesh):
    placed = (P(None, "row", "col", None, None), P(), P(None, "row", "col", None))
    return jax.shard_map(
        local,
        mesh=mesh,
        in_specs=placed,
        out_specs=P(None, "row", None, None, "col", None),
        check_vma=False,
    )
```
